256 devices in a mesh: region: 32 (over z, y), frac: 8 (over x, core).
Axes of the slice: x: 4, y: 4, z: 8, core: 2. Of those that a mesh axis runs over, the one named last changes fastest.
Arguments:
- pres_old: float32 [32, 32, 1024], P('region', None, 'frac'), may hold values from -6 to 6
- satur_old: float32 [32, 32, 1024], P('region', None, 'frac'), may hold values from 0.1 to 0.9
- permeability: float32 [32, 32, 1024], P('region', None, 'frac'), may hold values from 0.1 to 10
- storage: float32 [2, 32, 32, 1024], P(None, 'region', None, 'frac'), may hold values from 0.5 to 2
- source: float32 [2, 32, 32, 1024], P(None, 'region', None, 'frac'), may hold values from -4 to 4
- face_upwind: int32 [3, 32, 32, 1024], P(None, 'region', None, 'frac'), may hold values 0 or 1
- frac_pres_old: float32 [262144], P(('region', 'frac')), may hold values from -6 to 6
- frac_satur_old: float32 [262144], P(('region', 'frac')), may hold values from 0.1 to 0.9
- frac_storage: float32 [2, 262144], P(None, ('region', 'frac')), may hold values from 0.5 to 2
- frac_trans: float32 [262144], P(('region', 'frac')), may hold values from 1 to 10
- frac_upwind: int32 [262144], P(('region', 'frac')), may hold values 0 or 1
- coupling: float32 [4096, 64, 128], P(('region', 'frac')), may hold values from 0.002 to 0.05
- target_part: int32 [4096], P(('region', 'frac')), may hold values from 0 to 7
- target_row: int32 [4096], P(('region', 'frac')), may hold values from 0 to 31
- live_count: int32 [256], P(('region', 'frac')), may hold values from 4 to 16, as said below
Outputs:
- cell_state: float32 [2, 32, 32, 1024], P(None, 'region', None, 'frac')
- seg_state: float32 [2, 262144], P(None, ('region', 'frac'))
The draws below stay inside these ranges and needn't reach their ends.
Inputs may be any that keep to these rules, and one draw needn't show every extreme that they name: `live_count`: some device has all 16 slots live and some device has 4 live.
All inputs are finite; a program needn't handle non-finite values. No bound on the sum of `face_upwind` or of `frac_upwind` on one device may be relied on, other than what follows from the above.
Results may differ from the reference program's by a relative error of at most 0.0003.
Values sent between devices are 32-bit elements; how exact they have to be, the bound alone decides.
No kernel may reach another device: no remote copies, remote signals or barrier semaphores. Data moves between devices by JAX's collectives and lax.ppermute only.
A program may use at most 128 MiB of HBM per device.

```python
import math
import jax
import jax.numpy as jnp
from jax import lax

CZ = 1
CY = 32
CX = 128
SEG = 64
FB_DEV = 16
NEWTON = 2
SWEEPS = 5
GROUP = 8
ROWS = 32
NZ = 32
NY = 32
NX = 1024
NBLK = 4096
NSEG = 262144
N_FRAC = 8


def draw_live_count(key, part):
    fewest = max(FB_DEV // 4, 1)
    subkeys = jax.random.split(jax.random.fold_in(key, 17), 2)
    devices_all = NBLK // FB_DEV
    counts = jax.random.randint(subkeys[0], (devices_all,), fewest, FB_DEV + 1)
    shuffle = jax.random.permutation(subkeys[1], devices_all)
    counts = counts.at[shuffle[0]].set(FB_DEV)
    counts = counts.at[shuffle[1]].set(fewest)
    return counts.astype(jnp.int32)


def with_ends(values, stream_key, smallest, top_value):
    dims = values.shape
    index_at = [jax.random.randint(jax.random.fold_in(stream_key, axis), (), 0, dims[axis]) for axis in range(len(dims))]
    values = values.at[tuple(index_at)].set(smallest)
    longest = dims.index(max(dims))
    index_at[longest] = (index_at[longest] + 1) % dims[longest]
    return values.at[tuple(index_at)].set(top_value)


def block_levels(rng, extent, shards, least, largest):
    level = 1.0
    for dim, blocks in shards:
        steps = jax.random.uniform(jax.random.fold_in(jax.random.fold_in(rng, 6), dim), (blocks,), jnp.float32, least / len(shards), largest / len(shards))
        level = level * jnp.repeat(jnp.exp(steps), extent[dim] // blocks).reshape((-1,) + (1,) * (len(extent) - 1 - dim))
    return level


def bell_draw(rng, extent, scale, limit, cuts=(), held_as=jnp.bfloat16):
    array = scale * jax.random.normal(rng, extent, jnp.float32)
    if cuts:
        array = array * block_levels(rng, extent, cuts, -0.22, 0.18)
    return jnp.clip(array, -limit, limit).astype(held_as)


def setup_inputs(seed: int = 0) -> dict:
    keys = jax.random.split(jax.random.key(seed), 16)
    pres_old = bell_draw(keys[0], (NZ, NY, NX), 1.0, 6.0, ((0, 32), (2, 8)), jnp.float32)
    satur_old = jnp.clip(0.1 + 0.79999997 * jax.random.uniform(keys[1], (NZ, NY, NX), jnp.float32) ** block_levels(keys[1], (NZ, NY, NX), ((0, 32), (2, 8)), -0.2, 0.2), 0.1, 0.9)
    permeability = jnp.clip(jnp.exp(math.log(10.0) - 4.6051702 * jax.random.uniform(keys[2], (NZ, NY, NX), jnp.float32) ** block_levels(keys[2], (NZ, NY, NX), ((0, 32), (2, 8)), -0.2, 0.2)), 0.1, 10.0)
    storage = jnp.clip(jnp.exp(math.log(2.0) - 1.3862944 * jax.random.uniform(keys[3], (2, NZ, NY, NX), jnp.float32) ** block_levels(keys[3], (2, NZ, NY, NX), ((1, 32), (3, 8)), -0.2, 0.2)), 0.5, 2.0)
    source = bell_draw(keys[4], (2, NZ, NY, NX), 0.5, 4.0, ((1, 32), (3, 8)), jnp.float32)
    face_upwind = with_ends((jax.random.randint(keys[5], (3, NZ, NY, NX), 0, 2) < 1).astype(jnp.int32), jax.random.fold_in(keys[5], 1), 0, 1)
    frac_pres_old = bell_draw(keys[6], (NSEG,), 1.0, 6.0, ((0, 256),), jnp.float32)
    frac_satur_old = jnp.clip(0.1 + 0.79999997 * jax.random.uniform(keys[7], (NSEG,), jnp.float32) ** block_levels(keys[7], (NSEG,), ((0, 256),), -0.2, 0.2), 0.1, 0.9)
    frac_storage = jnp.clip(jnp.exp(math.log(2.0) - 1.3862944 * jax.random.uniform(keys[8], (2, NSEG), jnp.float32) ** block_levels(keys[8], (2, NSEG), ((1, 256),), -0.2, 0.2)), 0.5, 2.0)
    frac_trans = jnp.clip(jnp.exp(math.log(10.0) - 2.3025851 * jax.random.uniform(keys[9], (NSEG,), jnp.float32) ** block_levels(keys[9], (NSEG,), ((0, 256),), -0.2, 0.2)), 1.0, 10.0)
    frac_upwind = with_ends((jax.random.randint(keys[10], (NSEG,), 0, 2) < 1).astype(jnp.int32), jax.random.fold_in(keys[10], 1), 0, 1)
    coupling = jnp.clip(jnp.exp(math.log(0.05) - 3.218876 * jax.random.uniform(keys[11], (NBLK, SEG, CX), jnp.float32) ** block_levels(keys[11], (NBLK, SEG, CX), ((0, 256),), -0.2, 0.2)), 0.002, 0.05)
    target_part = with_ends(jax.random.randint(keys[12], (NBLK,), 0, GROUP), jax.random.fold_in(keys[12], 1), 0, GROUP - 1).astype(jnp.int32)
    target_row = with_ends(jax.random.randint(keys[13], (NBLK,), 0, ROWS), jax.random.fold_in(keys[13], 1), 0, ROWS - 1).astype(jnp.int32)
    live_count = draw_live_count(jax.random.fold_in(keys[15], 71), 0)
    return dict(pres_old=pres_old, satur_old=satur_old, permeability=permeability, storage=storage, source=source, face_upwind=face_upwind, frac_pres_old=frac_pres_old, frac_satur_old=frac_satur_old, frac_storage=frac_storage, frac_trans=frac_trans, frac_upwind=frac_upwind, coupling=coupling, target_part=target_part, target_row=target_row, live_count=live_count)


HIGHEST = lax.Precision.HIGHEST
VISCOSITY_RATIO = 0.5
TINY = 1e-06

def mobility(satur):
    water_mob = satur * satur
    total_mob = water_mob + VISCOSITY_RATIO * (1.0 - satur) * (1.0 - satur)
    return (water_mob, total_mob)

def harmonic(left_val, right_val):
    return 2.0 * left_val * right_val / (left_val + right_val)

def face_trans(perm_pad):
    trans_z = harmonic(perm_pad[:-1, 1:-1, 1:-1], perm_pad[1:, 1:-1, 1:-1])
    trans_y = harmonic(perm_pad[1:-1, :-1, 1:-1], perm_pad[1:-1, 1:, 1:-1])
    trans_x = harmonic(perm_pad[1:-1, 1:-1, :-1], perm_pad[1:-1, 1:-1, 1:])
    return (trans_z, trans_y, trans_x)

def directed(pres_left, pres_right, satur_left, satur_right, upwind, trans_face):
    satur_up = jnp.where(upwind == 1, satur_left, satur_right)
    water_mob, total_mob = mobility(satur_up)
    cond_total = trans_face * total_mob
    cond_water = trans_face * water_mob
    pres_drop = pres_left - pres_right
    return (cond_total * pres_drop, cond_water * pres_drop, cond_total, cond_water)

def net_faces(parts, member, sign):
    flux_z = parts[0][member]
    flux_y = parts[1][member]
    flux_x = parts[2][member]
    return flux_z[1:] + sign * flux_z[:-1] + (flux_y[:, 1:] + sign * flux_y[:, :-1]) + (flux_x[:, :, 1:] + sign * flux_x[:, :, :-1])

def cell_flux(pres_pad, satur_pad, flag_pad, trans_faces):
    trans_z, trans_y, trans_x = trans_faces
    along_z = directed(pres_pad[:-1, 1:-1, 1:-1], pres_pad[1:, 1:-1, 1:-1], satur_pad[:-1, 1:-1, 1:-1], satur_pad[1:, 1:-1, 1:-1], flag_pad[0, :-1, 1:-1, 1:-1], trans_z)
    along_y = directed(pres_pad[1:-1, :-1, 1:-1], pres_pad[1:-1, 1:, 1:-1], satur_pad[1:-1, :-1, 1:-1], satur_pad[1:-1, 1:, 1:-1], flag_pad[1, 1:-1, :-1, 1:-1], trans_y)
    along_x = directed(pres_pad[1:-1, 1:-1, :-1], pres_pad[1:-1, 1:-1, 1:], satur_pad[1:-1, 1:-1, :-1], satur_pad[1:-1, 1:-1, 1:], flag_pad[2, 1:-1, 1:-1, :-1], trans_x)
    parts = (along_z, along_y, along_x)
    return (net_faces(parts, 0, -1.0), net_faces(parts, 1, -1.0), net_faces(parts, 2, 1.0), net_faces(parts, 3, 1.0))

def chain_net(values, sign):
    return jnp.pad(values, ((0, 0), (0, 1))) + sign * jnp.pad(values, ((0, 0), (1, 0)))

def seg_flux(seg_pres, seg_satur, seg_trans, seg_flags):
    chain = directed(seg_pres[:, :-1], seg_pres[:, 1:], seg_satur[:, :-1], seg_satur[:, 1:], seg_flags[:, :-1], seg_trans[:, :-1])
    return (chain_net(chain[0], -1.0), chain_net(chain[1], -1.0), chain_net(chain[2], 1.0), chain_net(chain[3], 1.0))

def couple(weight, row_pres, row_satur, seg_pres):
    water_mob, total_mob = mobility(row_satur)
    mobile = jnp.stack([total_mob, water_mob])
    vectors = jnp.concatenate([mobile * row_pres[None], mobile])
    reached = jnp.einsum('bac,gbc->gba', weight, vectors, precision=HIGHEST)
    inflow = reached[:2] - seg_pres[None] * reached[2:]
    colsum = lax.optimization_barrier(jnp.sum(weight, axis=1))
    returned = jnp.einsum('ba,bac->bc', seg_pres, weight, precision=HIGHEST)
    outflow = mobile * (row_pres * colsum - returned)[None]
    return (inflow, outflow)

def precondition(remain, store, diag_t, diag_w):
    first = remain[0] / (store[0] + diag_t)
    second = (remain[1] - diag_w * first) / store[1]
    return jnp.stack([first, second])

def tangent_pair(func, first_point, second_point):
    values, pullback = jax.vjp(func, first_point, second_point)
    zero_cot = jax.tree.map(jnp.zeros_like, values)
    _, pushforward = jax.vjp(pullback, zero_cot)

    def forward_map(first_dir, second_dir):
        return pushforward((first_dir, second_dir))[0]
    return (values, forward_map)

def reference(pres_old, satur_old, permeability, storage, source, face_upwind, frac_pres_old, frac_satur_old, frac_storage, frac_trans, frac_upwind, coupling, target_part, target_row, live_count):
    trans_faces = face_trans(jnp.pad(permeability, 1))
    flag_pad = jnp.pad(face_upwind, ((0, 0), (1, 1), (1, 1), (1, 1)))
    blocks = coupling.shape[0]
    block_ids = jnp.arange(blocks, dtype=jnp.int32)
    owner_dev = block_ids // FB_DEV
    live_mask = (block_ids % FB_DEV < live_count[owner_dev]).astype(jnp.float32)
    weights = coupling * live_mask[:, None, None]
    zplane = owner_dev // N_FRAC * CZ + target_row // CY
    y_line = target_row % CY
    x_columns = target_part[:, None] * CX + jnp.arange(CX, dtype=jnp.int32)[None, :]
    seg_trans = frac_trans.reshape(blocks, SEG)
    seg_flags = frac_upwind.reshape(blocks, SEG)
    seg_store = frac_storage.reshape(2, blocks, SEG)
    live_segment = live_mask[None, :, None]
    old_cells = jnp.stack([pres_old, satur_old])
    old_segs = jnp.stack([frac_pres_old, frac_satur_old]).reshape(2, blocks, SEG)

    def residual(cell_now, seg_now):
        div_t, div_w, _, _ = cell_flux(jnp.pad(cell_now[0], 1), jnp.pad(cell_now[1], 1), flag_pad, trans_faces)
        row_pres = cell_now[0][zplane[:, None], y_line[:, None], x_columns]
        row_satur = cell_now[1][zplane[:, None], y_line[:, None], x_columns]
        inflow, outflow = couple(weights, row_pres, row_satur, seg_now[0])
        empty_grid = jnp.zeros(cell_now.shape[1:], jnp.float32)
        outflow_t = empty_grid.at[zplane[:, None], y_line[:, None], x_columns].add(outflow[0])
        outflow_w = empty_grid.at[zplane[:, None], y_line[:, None], x_columns].add(outflow[1])
        cell_div = jnp.stack([div_t + outflow_t, div_w + outflow_w])
        chain_t, chain_w, _, _ = seg_flux(seg_now[0], seg_now[1], seg_trans, seg_flags)
        seg_div = jnp.stack([chain_t, chain_w]) - inflow
        res_cells = storage * (cell_now - old_cells) + cell_div - source
        res_segs = live_segment * (seg_store * (seg_now - old_segs) + seg_div)
        return (res_cells, res_segs)
    cell_now = old_cells
    seg_now = old_segs
    for newton in range(NEWTON):
        (res_cells, res_segs), linear = tangent_pair(residual, cell_now, seg_now)
        _, _, diag_t, diag_w = cell_flux(jnp.pad(cell_now[0], 1), jnp.pad(cell_now[1], 1), flag_pad, trans_faces)
        _, _, chain_dt, chain_dw = seg_flux(seg_now[0], seg_now[1], seg_trans, seg_flags)
        remain_cell = -res_cells
        remain_seg = -res_segs
        step_cell = jnp.zeros_like(cell_now)
        step_seg = jnp.zeros_like(seg_now)
        for sweep_index in range(SWEEPS):
            dir_cell = precondition(remain_cell, storage, diag_t, diag_w)
            dir_seg = precondition(remain_seg, seg_store, chain_dt, chain_dw)
            image_cell, image_seg = linear(dir_cell, dir_seg)
            cross_sum = jnp.sum(remain_cell * image_cell) + jnp.sum(remain_seg * image_seg)
            square = jnp.sum(image_cell * image_cell) + jnp.sum(image_seg * image_seg)
            step_size = cross_sum / (square + TINY)
            step_cell = step_cell + step_size * dir_cell
            step_seg = step_seg + step_size * dir_seg
            remain_cell = remain_cell - step_size * image_cell
            remain_seg = remain_seg - step_size * image_seg
        cell_now = cell_now + step_cell
        seg_now = seg_now + step_seg
    return (cell_now, seg_now.reshape(2, blocks * SEG))
```

```python
import jax
import jax.numpy as jnp
from jax import lax
from jax.experimental import pallas as pl
from jax.experimental.pallas import tpu as pltpu
from jax.sharding import PartitionSpec as P

NEWTON = 2
SWEEPS = 5
VISCOSITY_RATIO = 0.5
TINY = 1e-06
SCALE = 1.0 / 16.0
UNROLL = 4
PAIRS = [(i, j) for i in range(SWEEPS + 1) for j in range(i, SWEEPS + 1)]
DOTS = 24
F32 = jnp.float32
VMEM_LIMIT = 24 * 2**20


def vmem(*shape):
    return pltpu.VMEM(shape, F32)


def smem_i32(*shape):
    return jax.ShapeDtypeStruct(shape, jnp.int32)


def call(body, outs, args, spaces, scratch=(), out_spaces=None, flops=20000, name=None):
    ins = []
    for arg, space in zip(args, spaces):
        if space == "v":
            arg = pltpu.with_memory_space_constraint(arg, pltpu.VMEM)
        ins.append(arg)
    kinds = {"v": pltpu.VMEM, "s": pltpu.SMEM, "a": pl.ANY}
    out_spaces = out_spaces or "v" * len(outs)
    return pl.pallas_call(
        body,
        out_shape=list(outs),
        in_specs=[pl.BlockSpec(memory_space=kinds[s]) for s in spaces],
        out_specs=[pl.BlockSpec(memory_space=kinds[s]) for s in out_spaces],
        scratch_shapes=list(scratch),
        compiler_params=pltpu.CompilerParams(vmem_limit_bytes=VMEM_LIMIT),
        cost_estimate=pl.CostEstimate(flops=flops, bytes_accessed=flops, transcendentals=0),
        name=name,
    )(*ins)


def mobility(satur):
    water_mob = satur * satur
    total_mob = water_mob + VISCOSITY_RATIO * (1.0 - satur) * (1.0 - satur)
    return water_mob, total_mob


def slopes(satur):
    return 2.0 * satur, 2.0 * satur - 2.0 * VISCOSITY_RATIO * (1.0 - satur)


def neighbours(own, below, above, left, right):
    lane = lax.broadcasted_iota(jnp.int32, own.shape, 1)
    x_next = jnp.where(lane == 127, pltpu.roll(right, 127, 1), pltpu.roll(own, 127, 1))
    x_prev = jnp.where(lane == 0, pltpu.roll(left, 1, 1), pltpu.roll(own, 1, 1))
    return (above, below, pltpu.roll(own, 31, 0), pltpu.roll(own, 1, 0), x_next, x_prev)


def chain_neighbours(own):
    return (pltpu.roll(own, 63, 0), pltpu.roll(own, 1, 0))


def harmonic(left_val, right_val):
    return 2.0 * left_val * right_val / (left_val + right_val)


def geometry(ids, own, below, above, left, right, flag_y, faces_ref, own_up_ref):
    region, frac, regions, fracs = ids[0], ids[1], ids[2], ids[3]
    block = [r[...] for r in (own, below, above, left, right)]
    perm = neighbours(*[b[64:96] for b in block])
    row = lax.broadcasted_iota(jnp.int32, (32, 128), 0)
    lane = lax.broadcasted_iota(jnp.int32, (32, 128), 1)
    everywhere = row >= 0
    inside = (
        everywhere & (region < regions - 1),
        everywhere & (region > 0),
        row < 31,
        row > 0,
        (lane < 127) | (frac < fracs - 1),
        (lane > 0) | (frac > 0),
    )
    here = block[0][64:96]
    for f in range(6):
        faces_ref[32 * f : 32 * f + 32] = jnp.where(inside[f], harmonic(here, perm[f]), 0.0)
    flag_z = block[0][96:128]
    flag_x = block[0][128:160]
    y_here = flag_y[...].astype(F32)
    z_prev = block[1][96:128]
    y_prev = pltpu.roll(y_here, 1, 0)
    x_prev = neighbours(flag_x, flag_x, flag_x, block[3][128:160], flag_x)[5]
    for f, (flag, forward) in enumerate(
        ((flag_z, 1), (z_prev, 0), (y_here, 1), (y_prev, 0), (flag_x, 1), (x_prev, 0))
    ):
        upstream = jnp.where(flag == 1.0, 1.0, 0.0)
        own_up_ref[32 * f : 32 * f + 32] = upstream if forward else 1.0 - upstream


def collect(
    ids, codes, *refs
):
    pieces = refs[:8]
    record = refs[8]
    weights, slots, rows, count, seg_old, seg_face, seg_up, seg_store, seg_live, sems = refs[9:]
    me = ids[1]
    blocks = 128

    def source(owner, slot, act):
        other = lax.rem(owner + me, 2)
        base = jnp.where(other == 1, me + 1 - 2 * lax.rem(me, 2), me)
        turn = lax.rem(base - owner + 8, 8) // 2
        which = other * 4 + turn
        for k in range(8):

            @pl.when(which == k)
            def _():
                act(pieces[k].at[slot])

    def visit(b, n):
        mine = (codes[b] >= 0) & (codes[b] // 32 == me)

        @pl.when(mine)
        def _():
            slots[n] = b
            rows[n] = lax.rem(codes[b], 32)
            source(
                b // 16,
                lax.rem(b, 16),
                lambda src: pltpu.make_async_copy(src, weights.at[n], sems.at[n]).start(),
            )

        return n + mine.astype(jnp.int32)

    n = lax.fori_loop(0, blocks, visit, jnp.int32(0))
    rounds = (n + UNROLL - 1) // UNROLL
    count[0] = rounds

    def fill(i, carry):
        slots[i] = -1
        rows[i] = 0
        pltpu.make_async_copy(pieces[0].at[0], weights.at[i], sems.at[i]).start()
        return carry

    lax.fori_loop(n, rounds * UNROLL, fill, 0)

    turned = [record[:, 128 * k : 128 * k + 128].T for k in range(4)]
    seg_old[...] = turned[0]
    trans, flags = turned[1][:64], turned[1][64:]
    at = lax.broadcasted_iota(jnp.int32, (64, 128), 0)
    seg_face[:64] = jnp.where(at < 63, trans, 0.0)
    seg_face[64:] = jnp.where(at > 0, pltpu.roll(trans, 1, 0), 0.0)
    upstream = jnp.where(flags == 1.0, 1.0, 0.0)
    seg_up[:64] = upstream
    seg_up[64:] = 1.0 - pltpu.roll(upstream, 1, 0)
    seg_store[...] = turned[2]
    code = turned[3][:8]
    first = (me * 32).astype(F32)
    seg_live[...] = jnp.where((code >= first) & (code < first + 32.0), 1.0, 0.0)

    def settle(i, carry):
        pltpu.make_async_copy(pieces[0].at[0], weights.at[i], sems.at[i]).wait()
        return carry

    lax.fori_loop(0, rounds * UNROLL, settle, 0)


def over_blocks(slots, rows, count, weights, lines, q, sums, returned, columns):
    lane = lax.broadcasted_iota(jnp.int32, (64, 128), 1)
    sums[...] = jnp.zeros_like(sums)
    returned[...] = jnp.zeros_like(returned)
    if columns is not None:
        columns[...] = jnp.zeros_like(columns)

    def body(step, carry):
        added = [jnp.zeros((64, 128), F32) for _ in range(4)]
        q_all = q[:64]
        backs = []
        for k in range(UNROLL):
            i = step * UNROLL + k
            slot, row = slots[i], rows[i]
            weight = weights[i]
            here = lane == slot
            for v in range(4):
                line = lines[pl.ds(32 * v + row, 1), :]
                total = jnp.sum(weight * line, axis=1, keepdims=True)
                added[v] = added[v] + jnp.where(here, total, 0.0)
            q_col = jnp.sum(jnp.where(here, q_all, 0.0), axis=1, keepdims=True)
            back = jnp.sum(weight * q_col, axis=0, keepdims=True)
            col = None
            if columns is not None:
                valid = jnp.where(slot >= 0, 1.0, 0.0)
                col = jnp.sum(weight, axis=0, keepdims=True) * valid
            backs.append((row, back, col))
        for v in range(4):
            sums[64 * v : 64 * v + 64] += added[v]
        for row, back, col in backs:
            returned[pl.ds(row, 1), :] += back
            if columns is not None:
                columns[pl.ds(row, 1), :] += col
        return carry

    lax.fori_loop(0, count[0], body, 0)


def combine(dots):
    total = jnp.sum(dots, axis=1, keepdims=True)
    total = jnp.broadcast_to(total, (DOTS, 128))
    gram = {}
    for n, (i, j) in enumerate(PAIRS):
        gram[i, j] = gram[j, i] = jnp.broadcast_to(total[n : n + 1, :], (8, 128))
    one = jnp.ones((8, 128), F32)
    remain = [one]
    factors = [jnp.zeros((8, 128), F32) for _ in range(SWEEPS)]
    for sweep in range(SWEEPS):
        image = [(j + 1, value / SCALE) for j, value in enumerate(remain)]
        cross = sum(value * factor * gram[j, i] for j, value in enumerate(remain) for i, factor in image)
        square = sum(a * b * gram[i, j] for i, a in image for j, b in image)
        alpha = cross / (square + TINY)
        for j, value in enumerate(remain):
            factors[j] = factors[j] + alpha * value
        longer = remain + [jnp.zeros((8, 128), F32)]
        for i, factor in image:
            longer[i] = longer[i] - alpha * factor
        remain = longer
    return factors


def spread(factor, rows):
    return jnp.broadcast_to(factor[:1], (rows, 128))


def summed(parts_ref):
    total = parts_ref[0]
    for k in range(1, parts_ref.shape[0]):
        total = total + parts_ref[k]
    return total


def face_terms(pres, satur, pres_across, satur_across, faces, own_up, coef_ref, stride):
    div_t = div_w = diag_t = diag_w = None
    count = len(pres_across)
    rows = pres.shape[0]
    for f in range(count):
        trans = faces[rows * f : rows * f + rows]
        up = own_up[rows * f : rows * f + rows]
        s_up = jnp.where(up == 1.0, satur, satur_across[f])
        drop = pres - pres_across[f]
        water, total = mobility(s_up)
        water_slope, total_slope = slopes(s_up)
        cond_t, cond_w = trans * total, trans * water
        lean = trans * drop
        at = rows * f
        coef_ref[at : at + rows] = cond_t
        coef_ref[stride + at : stride + at + rows] = cond_w
        coef_ref[2 * stride + at : 2 * stride + at + rows] = total_slope * lean
        coef_ref[3 * stride + at : 3 * stride + at + rows] = water_slope * lean
        flux_t, flux_w = cond_t * drop, cond_w * drop
        if f == 0:
            div_t, div_w, diag_t, diag_w = flux_t, flux_w, cond_t, cond_w
        else:
            div_t, div_w = div_t + flux_t, div_w + flux_w
            diag_t, diag_w = diag_t + cond_t, diag_w + cond_w
    return div_t, div_w, diag_t, diag_w


def face_tangents(dp, ds, dp_across, ds_across, own_up, coef, stride):
    rows = dp.shape[0]
    out_t = out_w = None
    for f in range(len(dp_across)):
        at = rows * f
        up = own_up[at : at + rows]
        drop = dp - dp_across[f]
        ds_up = jnp.where(up == 1.0, ds, ds_across[f])
        part_t = coef[at : at + rows] * drop + coef[2 * stride + at : 2 * stride + at + rows] * ds_up
        part_w = (
            coef[stride + at : stride + at + rows] * drop
            + coef[3 * stride + at : 3 * stride + at + rows] * ds_up
        )
        out_t = part_t if f == 0 else out_t + part_t
        out_w = part_w if f == 0 else out_w + part_w
    return out_t, out_w


def linearise(newton, *refs):
    refs = list(refs)

    def take(n):
        out = refs[:n]
        del refs[:n]
        return out

    slots, rows, count = take(3)
    cell_old, store, source, faces, own_up = take(5)
    seg_old, seg_store, seg_face, seg_up, seg_live, weights = take(6)
    [cell_in] = take(1)
    around = take(4)
    [seg_in] = take(1)
    if newton:
        [parts] = take(1)
        dir_cells = take(SWEEPS)
        dir_segs = take(SWEEPS)
        dir_around = [take(4) for _ in range(SWEEPS)]
    base_cell, base_seg, dir_cell, dir_seg = take(4)
    coef, seg_coef, lead, seg_lead, lines, reach, couple_rows = take(7)
    if newton:
        cell_out, seg_out = take(2)
    inner_lines, sums, returned, columns = refs

    cell = cell_in[...]
    near = [r[...] for r in around]
    if newton:
        factors = combine(summed(parts))
        for j in range(SWEEPS):
            g = spread(factors[j], 64)
            cell = cell + g * dir_cells[j][...]
            near = [n + g * d[...] for n, d in zip(near, dir_around[j])]
        cell_out[...] = cell
        seg = seg_in[...]
        for j in range(SWEEPS):
            seg = seg + spread(factors[j], 128) * dir_segs[j][...]
        seg_out[...] = seg
        seg_ref = seg_out
    else:
        seg = seg_in[...]
        seg_ref = seg_in
    pres, satur = cell[:32], cell[32:]
    q, r = seg[:64], seg[64:]

    water, total = mobility(satur)
    water_slope, total_slope = slopes(satur)
    lines[0:32] = total
    lines[32:64] = water
    lines[64:96] = total_slope
    lines[96:128] = water_slope
    lines[128:160] = pres
    inner_lines[0:32] = total
    inner_lines[32:64] = water
    inner_lines[64:96] = total * pres
    inner_lines[96:128] = water * pres
    over_blocks(slots, rows, count, weights, inner_lines, seg_ref, sums, returned, columns)
    reach[...] = sums[0:128]
    column = columns[...]
    pull = pres * column - returned[...]
    couple_rows[0:32] = column
    couple_rows[32:64] = pull

    pres_across = neighbours(pres, *[n[:32] for n in near])
    satur_across = neighbours(satur, *[n[32:] for n in near])
    div_t, div_w, diag_t, diag_w = face_terms(
        pres, satur, pres_across, satur_across, faces, own_up, coef, 192
    )
    st, sw = store[:32], store[32:]
    moved = cell - cell_old[...]
    base_t = source[:32] - st * moved[:32] - div_t - total * pull
    base_w = source[32:] - sw * moved[32:] - div_w - water * pull
    lead_t = 1.0 / (st + diag_t)
    lead_w = 1.0 / sw
    lead[0:32] = lead_t
    lead[32:64] = diag_w
    lead[64:96] = lead_w
    base_cell[0:32] = base_t
    base_cell[32:64] = base_w
    first = base_t * lead_t
    dir_cell[0:32] = first
    dir_cell[32:64] = (base_w - diag_w * first) * lead_w

    chain_t, chain_w, chain_dt, chain_dw = face_terms(
        q, r, chain_neighbours(q), chain_neighbours(r), seg_face, seg_up, seg_coef, 128
    )
    live = jnp.broadcast_to(seg_live[:1], (64, 128))
    sst, ssw = seg_store[:64], seg_store[64:]
    shifted = seg - seg_old[...]
    inflow_t = sums[128:192] - q * sums[0:64]
    inflow_w = sums[192:256] - q * sums[64:128]
    seg_t = -live * (sst * shifted[:64] + chain_t - inflow_t)
    seg_w = -live * (ssw * shifted[64:] + chain_w - inflow_w)
    lead_t = 1.0 / (sst + chain_dt)
    lead_w = 1.0 / ssw
    seg_lead[0:64] = lead_t
    seg_lead[64:128] = chain_dw
    seg_lead[128:192] = lead_w
    base_seg[0:64] = seg_t
    base_seg[64:128] = seg_w
    first = seg_t * lead_t
    dir_seg[0:64] = first
    dir_seg[64:128] = (seg_w - chain_dw * first) * lead_w


def couple_dirs(
    slots, rows, count, dir_cell, dir_seg, seg, lines, reach, weights, inflow, returned, inner_lines, sums
):
    dp, ds = dir_cell[:32], dir_cell[32:]
    pres = lines[128:160]
    lean_t = lines[64:96] * ds
    lean_w = lines[96:128] * ds
    inner_lines[0:32] = lines[0:32] * dp + lean_t * pres
    inner_lines[32:64] = lines[32:64] * dp + lean_w * pres
    inner_lines[64:96] = lean_t
    inner_lines[96:128] = lean_w
    over_blocks(slots, rows, count, weights, inner_lines, dir_seg, sums, returned, None)
    q, dq = seg[:64], dir_seg[:64]
    inflow[0:64] = sums[0:64] - q * sums[128:192] - dq * reach[0:64]
    inflow[64:128] = sums[64:128] - q * sums[192:256] - dq * reach[64:128]


def advance(last, *refs):
    (
        dir_cell,
        below,
        above,
        left,
        right,
        dir_seg,
        inflow,
        returned,
        store,
        own_up,
        seg_store,
        seg_up,
        seg_live,
        coef,
        seg_coef,
        lead,
        seg_lead,
        lines,
        couple_rows,
    ) = refs[:19]
    next_cell, next_seg = refs[19:21]
    dp, ds = dir_cell[:32], dir_cell[32:]
    near = [n[...] for n in (below, above, left, right)]
    out_t, out_w = face_tangents(
        dp,
        ds,
        neighbours(dp, *[n[:32] for n in near]),
        neighbours(ds, *[n[32:] for n in near]),
        own_up,
        coef,
        192,
    )
    flow = dp * couple_rows[0:32] - returned[...]
    pull = ds * couple_rows[32:64]
    image_t = store[:32] * dp + out_t + lines[0:32] * flow + lines[64:96] * pull
    image_w = store[32:] * ds + out_w + lines[32:64] * flow + lines[96:128] * pull
    cell_t, cell_w = SCALE * image_t, SCALE * image_w
    next_cell[0:32] = cell_t
    next_cell[32:64] = cell_w

    dq, dr = dir_seg[:64], dir_seg[64:]
    chain_t, chain_w = face_tangents(
        dq, dr, chain_neighbours(dq), chain_neighbours(dr), seg_up, seg_coef, 128
    )
    live = jnp.broadcast_to(SCALE * seg_live[:1], (64, 128))
    seg_t = live * (seg_store[:64] * dq + chain_t - inflow[:64])
    seg_w = live * (seg_store[64:] * dr + chain_w - inflow[64:])
    next_seg[0:64] = seg_t
    next_seg[64:128] = seg_w
    if not last:
        next_dir, next_dir_seg = refs[21:23]
        first = cell_t * lead[0:32]
        next_dir[0:32] = first
        next_dir[32:64] = (cell_w - lead[32:64] * first) * lead[64:96]
        first = seg_t * seg_lead[0:64]
        next_dir_seg[0:64] = first
        next_dir_seg[64:128] = (seg_w - seg_lead[64:128] * first) * seg_lead[128:192]


def inner_products(*refs):
    cells, segs, out = refs[: SWEEPS + 1], refs[SWEEPS + 1 : 2 * SWEEPS + 2], refs[-1]
    lines = []
    for i, j in PAIRS:
        part = jnp.sum(cells[i][...] * cells[j][...], axis=0, keepdims=True)
        lines.append(part + jnp.sum(segs[i][...] * segs[j][...], axis=0, keepdims=True))
    lines.append(jnp.zeros((DOTS - len(PAIRS), 128), F32))
    total = jnp.concatenate(lines, axis=0)
    for k in range(out.shape[0]):
        out[k] = total


def add_parts(parts, out):
    total = summed(parts)
    for k in range(out.shape[0]):
        out[k] = total


def finish(*refs):
    parts, cell, seg, seg_old = refs[:4]
    dir_cells = refs[4 : 4 + SWEEPS]
    dir_segs = refs[4 + SWEEPS : 4 + 2 * SWEEPS]
    cell_out, moved = refs[4 + 2 * SWEEPS :]
    factors = combine(summed(parts))
    total = cell[...]
    shift = seg[...] - seg_old[...]
    for j in range(SWEEPS):
        total = total + spread(factors[j], 64) * dir_cells[j][...]
        shift = shift + spread(factors[j], 128) * dir_segs[j][...]
    cell_out[...] = total
    moved[...] = shift.T


def ring(block, axis, distance):
    count = lax.axis_size(axis)
    return lax.ppermute(block, axis, [(i, (i + distance) % count) for i in range(count)])


def swapped(block, axis):
    return lax.ppermute(block, axis, [(i, i ^ 1) for i in range(lax.axis_size(axis))])


def exchanged(block):
    return [
        ring(block, "region", 1),
        ring(block, "region", -1),
        ring(block, "frac", 1),
        ring(block, "frac", -1),
    ]


def reduced(parts):
    y_groups = [[4 * z + y for y in range(4)] for z in range(8)]
    z_groups = [[4 * z + y for z in range(8)] for y in range(4)]
    parts = lax.all_to_all(parts, "frac", 0, 0)
    [parts] = call(add_parts, [vmem(4, DOTS, 128)], [parts], "v")
    parts = lax.all_to_all(parts, "region", 0, 0, axis_index_groups=y_groups)
    [parts] = call(add_parts, [vmem(8, DOTS, 128)], [parts], "v")
    return lax.all_to_all(parts, "region", 0, 0, axis_index_groups=z_groups)


def on_device(
    pres_old,
    satur_old,
    permeability,
    storage,
    source,
    face_upwind,
    frac_pres_old,
    frac_satur_old,
    frac_storage,
    frac_trans,
    frac_upwind,
    coupling,
    target_part,
    target_row,
    live_count,
):
    blocks = coupling.shape[0]
    ids = jnp.stack(
        [
            lax.axis_index("region"),
            lax.axis_index("frac"),
            jnp.int32(lax.axis_size("region")),
            jnp.int32(lax.axis_size("frac")),
        ]
    ).astype(jnp.int32)
    cell_old = jnp.concatenate([pres_old[0], satur_old[0]], axis=0)
    message = jnp.concatenate(
        [
            cell_old,
            permeability[0],
            face_upwind[0, 0].astype(F32),
            face_upwind[2, 0].astype(F32),
        ],
        axis=0,
    )
    live = jnp.arange(blocks, dtype=jnp.int32) < live_count[0]
    code = jnp.where(live, target_part * 32 + target_row, -1)
    record = jnp.concatenate(
        [
            x.reshape(blocks, 64)
            for x in (
                frac_pres_old,
                frac_satur_old,
                frac_trans,
                frac_upwind.astype(F32),
                frac_storage[0],
                frac_storage[1],
            )
        ]
        + [jnp.broadcast_to(code.astype(F32)[:, None], (blocks, 128))],
        axis=1,
    )
    around = exchanged(message)
    same = [coupling] + [ring(coupling, "frac", 2 * k) for k in (1, 2, 3)]
    pieces = same + [swapped(x, "frac") for x in same]
    record_all = lax.all_gather(record, "frac", axis=0, tiled=True)
    codes = record_all[:, 384].astype(jnp.int32)

    faces, own_up = call(
        geometry,
        [vmem(192, 128), vmem(192, 128)],
        [ids, message, *around, face_upwind[1, 0]],
        "svvvvvv",
    )
    room = 8 * blocks + UNROLL
    weights, slots, rows, count, seg_old, seg_face, seg_up, seg_store, seg_live = call(
        collect,
        [
            vmem(room, 64, 128),
            smem_i32(room),
            smem_i32(room),
            smem_i32(1),
            vmem(128, 128),
            vmem(128, 128),
            vmem(128, 128),
            vmem(128, 128),
            vmem(8, 128),
        ],
        [ids, codes, *pieces, record_all],
        "ss" + "a" * 8 + "v",
        scratch=[pltpu.SemaphoreType.DMA((room,))],
        out_spaces="vsss" + "v" * 5,
    )
    lists = [slots, rows, count]
    store = storage.reshape(64, 128)
    wells = source.reshape(64, 128)
    inner = [vmem(128, 128), vmem(256, 128)]

    cell, seg = cell_old, seg_old
    near = [x[:64] for x in around]
    parts = None
    for newton in range(NEWTON):
        args = [
            *lists,
            cell_old,
            store,
            wells,
            faces,
            own_up,
            seg_old,
            seg_store,
            seg_face,
            seg_up,
            seg_live,
            weights,
            cell,
            *near,
            seg,
        ]
        outs = [
            vmem(64, 128),
            vmem(128, 128),
            vmem(64, 128),
            vmem(128, 128),
            vmem(768, 128),
            vmem(512, 128),
            vmem(96, 128),
            vmem(192, 128),
            vmem(160, 128),
            vmem(128, 128),
            vmem(64, 128),
        ]
        if newton:
            args += [parts, *dir_cells, *dir_segs, *[x for group in dir_around for x in group]]
            outs += [vmem(64, 128), vmem(128, 128)]
        made = call(
            lambda *refs, newton=newton: linearise(newton, *refs),
            outs,
            args,
            "sss" + "v" * (len(args) - 3),
            scratch=[*inner, vmem(32, 128), vmem(32, 128)],
            name="linearise",
        )
        base_cell, base_seg, dir_cell, dir_seg = made[:4]
        coef, seg_coef, lead, seg_lead, lines, reach, couple_rows = made[4:11]
        if newton:
            cell, seg = made[11:]
        base_cells, base_segs = [base_cell], [base_seg]
        dir_cells, dir_segs, dir_around = [], [], []
        for sweep in range(SWEEPS):
            last = sweep == SWEEPS - 1
            nearby = exchanged(dir_cell)
            inflow, returned = call(
                couple_dirs,
                [vmem(128, 128), vmem(32, 128)],
                [*lists, dir_cell, dir_seg, seg, lines, reach, weights],
                "sss" + "v" * 6,
                scratch=inner,
                name="couple",
            )
            dir_cells.append(dir_cell)
            dir_segs.append(dir_seg)
            dir_around.append(nearby)
            args = [
                dir_cell,
                *nearby,
                dir_seg,
                inflow,
                returned,
                store,
                own_up,
                seg_store,
                seg_up,
                seg_live,
                coef,
                seg_coef,
                lead,
                seg_lead,
                lines,
                couple_rows,
            ]
            made = call(
                lambda *refs, last=last: advance(last, *refs),
                [vmem(64, 128), vmem(128, 128)] * (1 if last else 2),
                args,
                "v" * len(args),
                name="advance",
            )
            base_cells.append(made[0])
            base_segs.append(made[1])
            if not last:
                dir_cell, dir_seg = made[2:]
        [parts] = call(
            inner_products,
            [vmem(8, DOTS, 128)],
            [*base_cells, *base_segs],
            "v" * (2 * SWEEPS + 2),
            name="inner_products",
        )
        parts = reduced(parts)

    args = [parts, cell, seg, seg_old, *dir_cells, *dir_segs]
    cell_state, moved = call(
        finish,
        [jax.ShapeDtypeStruct((64, 128), F32), vmem(128, 128)],
        args,
        "v" * len(args),
        name="finish",
    )
    moved = lax.all_to_all(moved.reshape(8, blocks, 128), "frac", 0, 0)
    moved = jnp.sum(moved, axis=0)
    seg_state = jnp.stack(
        [
            frac_pres_old + moved[:, :64].reshape(-1),
            frac_satur_old + moved[:, 64:].reshape(-1),
        ]
    )
    return (cell_state.reshape(2, 1, 32, 128), seg_state)


def solution(mesh):
    placed = (
        P("region", None, "frac"),
        P("region", None, "frac"),
        P("region", None, "frac"),
        P(None, "region", None, "frac"),
        P(None, "region", None, "frac"),
        P(None, "region", None, "frac"),
        P(("region", "frac")),
        P(("region", "frac")),
        P(None, ("region", "frac")),
        P(("region", "frac")),
        P(("region", "frac")),
        P(("region", "frac"), None, None),
        P(("region", "frac")),
        P(("region", "frac")),
        P(("region", "frac")),
    )
    return jax.shard_map(
        on_device,
        mesh=mesh,
        in_specs=placed,
        out_specs=(P(None, "region", None, "frac"), P(None, ("region", "frac"))),
        check_vma=False,
    )
```

```python
import jax
import jax.numpy as jnp
from jax import lax
from jax.experimental import pallas as pl
from jax.experimental.pallas import tpu as pltpu
from jax.sharding import PartitionSpec as P

NEWTON = 2
SWEEPS = 5
VISCOSITY_RATIO = 0.5
TINY = 1e-06
SCALE = 1.0 / 16.0
UNROLL = 4
PAIRS = [(i, j) for i in range(SWEEPS + 1) for j in range(i, SWEEPS + 1)]
F32 = jnp.float32
VMEM_LIMIT = 24 * 2**20


def vmem(*shape):
    return pltpu.VMEM(shape, F32)


def smem_i32(*shape):
    return pltpu.SMEM(shape, jnp.int32)


def call(body, outs, args, spaces, scratch=(), out_spaces=None, flops=20000, name=None):
    ins = []
    for arg, space in zip(args, spaces):
        if space == "v":
            arg = pltpu.with_memory_space_constraint(arg, pltpu.VMEM)
        elif space == "H":
            arg = pltpu.with_memory_space_constraint(arg, pltpu.HBM)
        elif space == "S":
            arg = pltpu.with_memory_space_constraint(arg, pltpu.SMEM)
        ins.append(arg)
    kinds = {"v": pltpu.VMEM, "h": pltpu.VMEM, "s": pltpu.SMEM, "S": pltpu.SMEM, "a": pl.ANY, "H": pltpu.HBM}
    out_spaces = out_spaces or "v" * len(outs)
    return pl.pallas_call(
        body,
        out_shape=list(outs),
        in_specs=[pl.BlockSpec(memory_space=kinds[s]) for s in spaces],
        out_specs=[pl.BlockSpec(memory_space=kinds[s]) for s in out_spaces],
        scratch_shapes=list(scratch),
        compiler_params=pltpu.CompilerParams(vmem_limit_bytes=VMEM_LIMIT),
        cost_estimate=pl.CostEstimate(flops=flops, bytes_accessed=flops, transcendentals=0),
        name=name,
    )(*ins)


def mobility(satur):
    water_mob = satur * satur
    total_mob = water_mob + VISCOSITY_RATIO * (1.0 - satur) * (1.0 - satur)
    return water_mob, total_mob


def slopes(satur):
    return 2.0 * satur, 2.0 * satur - 2.0 * VISCOSITY_RATIO * (1.0 - satur)


def neighbours(own, below, above, left, right):
    lane = lax.broadcasted_iota(jnp.int32, own.shape, 1)
    x_next = jnp.where(lane == 127, pltpu.roll(right, 127, 1), pltpu.roll(own, 127, 1))
    x_prev = jnp.where(lane == 0, pltpu.roll(left, 1, 1), pltpu.roll(own, 1, 1))
    return (above, below, pltpu.roll(own, 31, 0), pltpu.roll(own, 1, 0), x_next, x_prev)


def chain_neighbours(own):
    return (pltpu.roll(own, 63, 0), pltpu.roll(own, 1, 0))


def harmonic(left_val, right_val):
    return 2.0 * left_val * right_val / (left_val + right_val)


def geometry(ids, own, below, above, left, right, flag_y, faces_ref, own_up_ref):
    region, frac, regions, fracs = ids[0], ids[1], ids[2], ids[3]
    block = [r[...] for r in (own, below, above, left, right)]
    perm = neighbours(*[b[64:96] for b in block])
    row = lax.broadcasted_iota(jnp.int32, (32, 128), 0)
    lane = lax.broadcasted_iota(jnp.int32, (32, 128), 1)
    everywhere = row >= 0
    inside = (
        everywhere & (region < regions - 1),
        everywhere & (region > 0),
        row < 31,
        row > 0,
        (lane < 127) | (frac < fracs - 1),
        (lane > 0) | (frac > 0),
    )
    here = block[0][64:96]
    for f in range(6):
        faces_ref[32 * f : 32 * f + 32] = jnp.where(inside[f], harmonic(here, perm[f]), 0.0)
    flag_z = block[0][96:128]
    flag_x = block[0][128:160]
    y_here = flag_y[...]
    z_prev = block[1][96:128]
    y_prev = pltpu.roll(y_here, 1, 0)
    x_prev = neighbours(flag_x, flag_x, flag_x, block[3][128:160], flag_x)[5]
    for f, (flag, forward) in enumerate(
        ((flag_z, 1), (z_prev, 0), (y_here, 1), (y_prev, 0), (flag_x, 1), (x_prev, 0))
    ):
        upstream = jnp.where(flag == 1.0, 1.0, 0.0)
        own_up_ref[32 * f : 32 * f + 32] = upstream if forward else 1.0 - upstream


def pack(
    ids, parts, rows, live, pres, satur, perm, flags, q, r, trans, ups, store,
    ids_out, message, record, cell, flag_y, flag_room, up_room, store_room, sems,
):
    copies = [
        pltpu.make_async_copy(src, dst, sems.at[n])
        for n, (src, dst) in enumerate(
            (
                (pres.at[0], cell.at[0:32]),
                (satur.at[0], cell.at[32:64]),
                (perm.at[0], message.at[64:96]),
                (flags, flag_room),
                (q, record.at[0:8]),
                (r, record.at[8:16]),
                (trans, record.at[16:24]),
                (ups, up_room),
                (store, store_room),
            )
        )
    ]
    for copy in copies:
        copy.start()
    for k in range(4):
        ids_out[k] = ids[k]
    lane = lax.broadcasted_iota(jnp.int32, (8, 128), 1)
    codes = jnp.full((8, 128), -1.0, F32)
    for k in range(16):
        code = jnp.where(k < live[0], parts[k] * 32 + rows[k], -1)
        codes = jnp.where(lane == k, code.astype(F32), codes)
    record[48:56] = codes
    for copy in copies:
        copy.wait()
    message[0:64] = cell[...]
    message[96:128] = flag_room[0, 0].astype(F32)
    message[128:160] = flag_room[2, 0].astype(F32)
    flag_y[...] = flag_room[1, 0].astype(F32)
    record[24:32] = up_room[...].astype(F32)
    for k in range(8):
        for c in range(2):
            row = 32 + 8 * c + k
            record[row : row + 1] = store_room[c : c + 1, 128 * k : 128 * k + 128]
    first = message[0:128].T
    rest = jnp.concatenate([message[128:160], jnp.zeros((96, 128), F32)], axis=0).T
    record[56:57] = first[127:128]
    record[57:58] = rest[127:128]
    record[58:59] = first[0:1]
    record[59:60] = rest[0:1]
    record[60:64] = jnp.zeros((4, 128), F32)


def owner_of(piece, me):
    base = me if piece < 4 else me + 1 - 2 * (me & 1)
    return (base - 2 * (piece % 4) + 8) & 7


def halves(first, second):
    low = lax.broadcasted_iota(jnp.int32, first.shape, 1) < 64
    return (
        jnp.where(low, first, pltpu.roll(second, 64, 1)),
        jnp.where(low, pltpu.roll(first, 64, 1), second),
    )


def survey(
    ids, records,
    slots, rows, places, count, seg_old, seg_face, seg_up, seg_store, seg_live, left, right,
    code_room, codes, sem,
):
    me = ids[1]
    lane = lax.broadcasted_iota(jnp.int32, (8, 128), 1)
    places_of = [pl.multiple_of(owner_of(k, me) * 64, 64) for k in range(8)]
    for k in range(8):
        code_room[k : k + 1] = records[pl.ds(places_of[k] + 48, 8), :][:1].astype(jnp.int32)
    copy = pltpu.make_async_copy(code_room, codes, sem)
    copy.start()

    for side, owner, row in ((left, (me + 7) & 7, 0), (right, (me + 1) & 7, 2)):
        columns = records[pl.ds(pl.multiple_of(owner * 64, 64) + 56, 8), :]
        side[0:128] = jnp.broadcast_to(columns[row : row + 1], (128, 128)).T
        side[128:160] = jnp.broadcast_to(columns[row + 1 : row + 2], (128, 128)).T[:32]

    copy.wait()

    def visit(slot, carry):
        n, live = carry
        for k in range(8):
            code = codes[k, slot]
            mine = (code >> 5) == me
            place = (slot & 1) * 64 + 8 * k + (slot >> 1)
            slots[n] = place
            rows[n] = code & 31
            places[n] = 16 * k + slot
            live = jnp.where(lane == jnp.where(mine, place, -1), 1.0, live)
            n = n + jnp.where(mine, 1, 0)
        return n, live

    n, live = lax.fori_loop(0, 16, visit, (jnp.int32(0), jnp.zeros((8, 128), F32)))
    seg_live[...] = live
    count[0] = (n + UNROLL - 1) // UNROLL
    for k in range(UNROLL - 1):
        slots[n + k] = -1
        rows[n + k] = 0
        places[n + k] = 0

    def field(k):
        return jnp.concatenate([records[pl.ds(p + 8 * k, 8), :] for p in places_of], axis=0)

    def turned(k):
        both = jnp.concatenate([field(k), field(k + 1)], axis=0).T
        return halves(both[:64], both[64:])

    seg_old[:64], seg_old[64:] = turned(0)
    trans, flags = turned(2)
    at = lax.broadcasted_iota(jnp.int32, (64, 128), 0)
    seg_face[:64] = jnp.where(at < 63, trans, 0.0)
    seg_face[64:] = jnp.where(at > 0, pltpu.roll(trans, 1, 0), 0.0)
    upstream = jnp.where(flags == 1.0, 1.0, 0.0)
    seg_up[:64] = upstream
    seg_up[64:] = 1.0 - pltpu.roll(upstream, 1, 0)
    seg_store[:64], seg_store[64:] = turned(4)


def collect(places, count, *refs):
    pieces, weights, sems = refs[:10], refs[10], refs[11]
    starts = (0, 16, 32, 40, 48, 64, 80, 96, 104, 112, 128)

    def fetch(i, carry):
        place = places[i]
        for k in range(10):

            @pl.when((place >= starts[k]) & (place < starts[k + 1]))
            def _():
                pltpu.make_async_copy(pieces[k].at[place - starts[k]], weights.at[i], sems.at[i]).start()

        return carry

    def settle(i, carry):
        pltpu.make_async_copy(pieces[0].at[0], weights.at[i], sems.at[i]).wait()
        return carry

    lax.fori_loop(0, count[0] * UNROLL, fetch, 0)
    lax.fori_loop(0, count[0] * UNROLL, settle, 0)


def survey_blocks(slots, rows, count, weights, lines, q, sums, returned, columns, levels):
    lane = lax.broadcasted_iota(jnp.int32, (64, 128), 1)
    sums[...] = jnp.zeros_like(sums)
    returned[...] = jnp.zeros_like(returned)
    columns[...] = jnp.zeros_like(columns)

    def body(step, carry):
        added = [jnp.zeros((64, 128), F32) for _ in range(4)]
        q_all = q[:64]
        backs = []
        for k in range(UNROLL):
            i = step * UNROLL + k
            slot, row = slots[i], rows[i]
            weight = weights[i]
            here = lane == slot
            for v in range(4):
                line = lines[pl.ds(32 * v + row, 1), :]
                total = jnp.sum(weight * line, axis=1, keepdims=True)
                added[v] = added[v] + jnp.where(here, total, 0.0)
            q_col = jnp.sum(jnp.where(here, q_all, 0.0), axis=1, keepdims=True)
            levels[i] = jnp.broadcast_to(q_col, (64, 128))
            back = jnp.sum(weight * q_col, axis=0, keepdims=True)
            valid = jnp.where(slot >= 0, 1.0, 0.0)
            backs.append((row, back, jnp.sum(weight, axis=0, keepdims=True) * valid))
        for v in range(4):
            sums[64 * v : 64 * v + 64] += added[v]
        for row, back, col in backs:
            returned[pl.ds(row, 1), :] += back
            columns[pl.ds(row, 1), :] += col
        return carry

    lax.fori_loop(0, count[0], body, 0)


def couple_blocks(slots, rows, count, weights, levels, lines, dq, inflow, returned):
    lane = lax.broadcasted_iota(jnp.int32, (64, 128), 1)
    returned[...] = jnp.zeros_like(returned)

    def body(step, carry):
        added = [jnp.zeros((64, 128), F32) for _ in range(2)]
        dq_all = dq[:64]
        backs = []
        for k in range(UNROLL):
            i = step * UNROLL + k
            slot, row = slots[i], rows[i]
            weight, level = weights[i], levels[i]
            here = lane == slot
            for v in range(2):
                first = lines[pl.ds(32 * v + row, 1), :]
                second = lines[pl.ds(64 + 32 * v + row, 1), :]
                total = jnp.sum(weight * (first - level * second), axis=1, keepdims=True)
                added[v] = added[v] + jnp.where(here, total, 0.0)
            dq_col = jnp.sum(jnp.where(here, dq_all, 0.0), axis=1, keepdims=True)
            backs.append((row, jnp.sum(weight * dq_col, axis=0, keepdims=True)))
        for v in range(2):
            inflow[64 * v : 64 * v + 64] += added[v]
        for row, back in backs:
            returned[pl.ds(row, 1), :] += back
        return carry

    lax.fori_loop(0, count[0], body, 0)


def combine(dots):
    total = jnp.broadcast_to(dots, (128, 128)).T
    gram = {}
    for n, (i, j) in enumerate(PAIRS):
        gram[i, j] = gram[j, i] = jnp.broadcast_to(total[n : n + 1, :], (8, 128))
    one = jnp.ones((8, 128), F32)
    remain = [one]
    factors = [jnp.zeros((8, 128), F32) for _ in range(SWEEPS)]
    for sweep in range(SWEEPS):
        image = [(j + 1, value / SCALE) for j, value in enumerate(remain)]
        cross = sum(value * factor * gram[j, i] for j, value in enumerate(remain) for i, factor in image)
        square = sum(a * b * gram[i, j] for i, a in image for j, b in image)
        alpha = cross / (square + TINY)
        for j, value in enumerate(remain):
            factors[j] = factors[j] + alpha * value
        longer = remain + [jnp.zeros((8, 128), F32)]
        for i, factor in image:
            longer[i] = longer[i] - alpha * factor
        remain = longer
    return factors


def spread(factor, rows):
    return jnp.broadcast_to(factor[:1], (rows, 128))


def summed(parts_ref):
    return jnp.sum(parts_ref[...], axis=0)


def face_terms(pres, satur, pres_across, satur_across, faces, own_up, coef_ref, stride):
    div_t = div_w = diag_t = diag_w = None
    count = len(pres_across)
    rows = pres.shape[0]
    for f in range(count):
        trans = faces[rows * f : rows * f + rows]
        up = own_up[rows * f : rows * f + rows]
        s_up = jnp.where(up == 1.0, satur, satur_across[f])
        drop = pres - pres_across[f]
        water, total = mobility(s_up)
        water_slope, total_slope = slopes(s_up)
        cond_t, cond_w = trans * total, trans * water
        lean = trans * drop
        at = rows * f
        coef_ref[at : at + rows] = cond_t
        coef_ref[stride + at : stride + at + rows] = cond_w
        coef_ref[2 * stride + at : 2 * stride + at + rows] = total_slope * lean
        coef_ref[3 * stride + at : 3 * stride + at + rows] = water_slope * lean
        flux_t, flux_w = cond_t * drop, cond_w * drop
        if f == 0:
            div_t, div_w, diag_t, diag_w = flux_t, flux_w, cond_t, cond_w
        else:
            div_t, div_w = div_t + flux_t, div_w + flux_w
            diag_t, diag_w = diag_t + cond_t, diag_w + cond_w
    return div_t, div_w, diag_t, diag_w


def face_tangents(dp, ds, dp_across, ds_across, own_up, coef, stride):
    rows = dp.shape[0]
    out_t = out_w = None
    for f in range(len(dp_across)):
        at = rows * f
        up = own_up[at : at + rows]
        drop = dp - dp_across[f]
        ds_up = jnp.where(up == 1.0, ds, ds_across[f])
        part_t = coef[at : at + rows] * drop + coef[2 * stride + at : 2 * stride + at + rows] * ds_up
        part_w = (
            coef[stride + at : stride + at + rows] * drop
            + coef[3 * stride + at : 3 * stride + at + rows] * ds_up
        )
        out_t = part_t if f == 0 else out_t + part_t
        out_w = part_w if f == 0 else out_w + part_w
    return out_t, out_w


def linearise(newton, *refs):
    refs = list(refs)

    def take(n):
        out = refs[:n]
        del refs[:n]
        return out

    slots, rows, count = take(3)
    cell_old, store, source, faces, own_up = take(5)
    seg_old, seg_store, seg_face, seg_up, seg_live, weights = take(6)
    [cell_in] = take(1)
    around = take(4)
    [seg_in] = take(1)
    if newton:
        [parts] = take(1)
        dir_cells = take(SWEEPS)
        dir_segs = take(SWEEPS)
        dir_around = [take(4) for _ in range(SWEEPS)]
    base_cell, base_seg, dir_cell, dir_seg = take(4)
    coef, seg_coef, lead, seg_lead, lines, reach, couple_rows, levels = take(8)
    if newton:
        cell_out, seg_out = take(2)
    inner_lines, sums, returned, columns = refs

    cell = cell_in[...]
    near = [r[0:64] for r in around]
    if newton:
        factors = combine(summed(parts))
        for j in range(SWEEPS):
            g = spread(factors[j], 64)
            cell = cell + g * dir_cells[j][...]
            near = [n + g * d[...] for n, d in zip(near, dir_around[j])]
        cell_out[...] = cell
        seg = seg_in[...]
        for j in range(SWEEPS):
            seg = seg + spread(factors[j], 128) * dir_segs[j][...]
        seg_out[...] = seg
        seg_ref = seg_out
    else:
        seg = seg_in[...]
        seg_ref = seg_in
    pres, satur = cell[:32], cell[32:]
    q, r = seg[:64], seg[64:]

    water, total = mobility(satur)
    water_slope, total_slope = slopes(satur)
    lines[0:32] = total
    lines[32:64] = water
    lines[64:96] = total_slope
    lines[96:128] = water_slope
    lines[128:160] = pres
    inner_lines[0:32] = total
    inner_lines[32:64] = water
    inner_lines[64:96] = total * pres
    inner_lines[96:128] = water * pres
    survey_blocks(slots, rows, count, weights, inner_lines, seg_ref, sums, returned, columns, levels)
    reach[...] = sums[0:128]
    column = columns[...]
    pull = pres * column - returned[...]
    couple_rows[0:32] = column
    couple_rows[32:64] = pull

    pres_across = neighbours(pres, *[n[:32] for n in near])
    satur_across = neighbours(satur, *[n[32:] for n in near])
    div_t, div_w, diag_t, diag_w = face_terms(
        pres, satur, pres_across, satur_across, faces, own_up, coef, 192
    )
    st, sw = store[:32], store[32:]
    moved = cell - cell_old[...]
    base_t = source[:32] - st * moved[:32] - div_t - total * pull
    base_w = source[32:] - sw * moved[32:] - div_w - water * pull
    lead_t = 1.0 / (st + diag_t)
    lead_w = 1.0 / sw
    lead[0:32] = lead_t
    lead[32:64] = diag_w
    lead[64:96] = lead_w
    base_cell[0:32] = base_t
    base_cell[32:64] = base_w
    first = base_t * lead_t
    dir_cell[0:32] = first
    dir_cell[32:64] = (base_w - diag_w * first) * lead_w

    chain_t, chain_w, chain_dt, chain_dw = face_terms(
        q, r, chain_neighbours(q), chain_neighbours(r), seg_face, seg_up, seg_coef, 128
    )
    live = jnp.broadcast_to(seg_live[:1], (64, 128))
    sst, ssw = seg_store[:64], seg_store[64:]
    shifted = seg - seg_old[...]
    inflow_t = sums[128:192] - q * sums[0:64]
    inflow_w = sums[192:256] - q * sums[64:128]
    seg_t = -live * (sst * shifted[:64] + chain_t - inflow_t)
    seg_w = -live * (ssw * shifted[64:] + chain_w - inflow_w)
    lead_t = 1.0 / (sst + chain_dt)
    lead_w = 1.0 / ssw
    seg_lead[0:64] = lead_t
    seg_lead[64:128] = chain_dw
    seg_lead[128:192] = lead_w
    base_seg[0:64] = seg_t
    base_seg[64:128] = seg_w
    first = seg_t * lead_t
    dir_seg[0:64] = first
    dir_seg[64:128] = (seg_w - chain_dw * first) * lead_w


def couple_dirs(
    slots, rows, count, dir_cell, dir_seg, lines, reach, weights, levels, inflow, returned, inner_lines
):
    dp, ds = dir_cell[:32], dir_cell[32:]
    pres = lines[128:160]
    lean_t = lines[64:96] * ds
    lean_w = lines[96:128] * ds
    inner_lines[0:32] = lines[0:32] * dp + lean_t * pres
    inner_lines[32:64] = lines[32:64] * dp + lean_w * pres
    inner_lines[64:96] = lean_t
    inner_lines[96:128] = lean_w
    dq = dir_seg[:64]
    inflow[0:64] = -dq * reach[0:64]
    inflow[64:128] = -dq * reach[64:128]
    couple_blocks(slots, rows, count, weights, levels, inner_lines, dir_seg, inflow, returned)


def advance(last, *refs):
    (
        dir_cell,
        below,
        above,
        left,
        right,
        dir_seg,
        inflow,
        returned,
        store,
        own_up,
        seg_store,
        seg_up,
        seg_live,
        coef,
        seg_coef,
        lead,
        seg_lead,
        lines,
        couple_rows,
    ) = refs[:19]
    next_cell, next_seg = refs[19:21]
    dp, ds = dir_cell[:32], dir_cell[32:]
    near = [n[...] for n in (below, above, left, right)]
    out_t, out_w = face_tangents(
        dp,
        ds,
        neighbours(dp, *[n[:32] for n in near]),
        neighbours(ds, *[n[32:] for n in near]),
        own_up,
        coef,
        192,
    )
    flow = dp * couple_rows[0:32] - returned[...]
    pull = ds * couple_rows[32:64]
    image_t = store[:32] * dp + out_t + lines[0:32] * flow + lines[64:96] * pull
    image_w = store[32:] * ds + out_w + lines[32:64] * flow + lines[96:128] * pull
    cell_t, cell_w = SCALE * image_t, SCALE * image_w
    next_cell[0:32] = cell_t
    next_cell[32:64] = cell_w

    dq, dr = dir_seg[:64], dir_seg[64:]
    chain_t, chain_w = face_tangents(
        dq, dr, chain_neighbours(dq), chain_neighbours(dr), seg_up, seg_coef, 128
    )
    live = jnp.broadcast_to(SCALE * seg_live[:1], (64, 128))
    seg_t = live * (seg_store[:64] * dq + chain_t - inflow[:64])
    seg_w = live * (seg_store[64:] * dr + chain_w - inflow[64:])
    next_seg[0:64] = seg_t
    next_seg[64:128] = seg_w
    if not last:
        next_dir, next_dir_seg = refs[21:23]
        first = cell_t * lead[0:32]
        next_dir[0:32] = first
        next_dir[32:64] = (cell_w - lead[32:64] * first) * lead[64:96]
        first = seg_t * seg_lead[0:64]
        next_dir_seg[0:64] = first
        next_dir_seg[64:128] = (seg_w - seg_lead[64:128] * first) * seg_lead[128:192]


def inner_products(*refs):
    cells, segs, out = refs[: SWEEPS + 1], refs[SWEEPS + 1 : 2 * SWEEPS + 2], refs[-1]
    lines = []
    for i, j in PAIRS:
        part = jnp.sum(cells[i][...] * cells[j][...], axis=0, keepdims=True)
        lines.append(part + jnp.sum(segs[i][...] * segs[j][...], axis=0, keepdims=True))
    lines.append(jnp.zeros((128 - len(PAIRS), 128), F32))
    total = jnp.sum(jnp.concatenate(lines, axis=0).T, axis=0, keepdims=True)
    out[...] = jnp.broadcast_to(total[None], out.shape)


def finish(*refs):
    ids, parts, cell, seg, seg_old = refs[:5]
    dir_cells = refs[5 : 5 + SWEEPS]
    dir_segs = refs[5 + SWEEPS : 5 + 2 * SWEEPS]
    cell_out, moved = refs[5 + 2 * SWEEPS :]
    factors = combine(summed(parts))
    total = cell[...]
    shift = seg[...] - seg_old[...]
    for j in range(SWEEPS):
        total = total + spread(factors[j], 64) * dir_cells[j][...]
        shift = shift + spread(factors[j], 128) * dir_segs[j][...]
    cell_out[...] = total
    turned = jnp.concatenate(halves(shift[:64], shift[64:]), axis=0).T
    me = ids[1]
    for k in range(8):
        owner = owner_of(k, me)
        moved[owner, 0:8] = turned[8 * k : 8 * k + 8]
        moved[owner, 8:16] = turned[64 + 8 * k : 64 + 8 * k + 8]


def ring(block, axis, distance):
    count = lax.axis_size(axis)
    return lax.ppermute(block, axis, [(i, (i + distance) % count) for i in range(count)])


def swapped(block, axis):
    return lax.ppermute(block, axis, [(i, i ^ 1) for i in range(lax.axis_size(axis))])


def exchanged(block):
    left, right = ring(block, "frac", 1), ring(block, "frac", -1)
    return [ring(block, "region", 1), ring(block, "region", -1), left, right]


def after(first, *others):
    return lax.optimization_barrier((first, *others))


def on_device(
    pres_old,
    satur_old,
    permeability,
    storage,
    source,
    face_upwind,
    frac_pres_old,
    frac_satur_old,
    frac_storage,
    frac_trans,
    frac_upwind,
    coupling,
    target_part,
    target_row,
    live_count,
):
    blocks = coupling.shape[0]
    ids = jnp.stack(
        [
            lax.axis_index("region"),
            lax.axis_index("frac"),
            jnp.int32(lax.axis_size("region")),
            jnp.int32(lax.axis_size("frac")),
        ]
    ).astype(jnp.int32)
    one_right = ring(coupling, "frac", 2)
    one_left = ring(coupling, "frac", -2)
    ids, message, record, cell_old, flag_y = call(
        pack,
        [smem_i32(4), vmem(160, 128), vmem(64, 128), vmem(64, 128), vmem(32, 128)],
        [
            ids,
            target_part,
            target_row,
            live_count,
            pres_old,
            satur_old,
            permeability,
            face_upwind,
            frac_pres_old.reshape(8, 128),
            frac_satur_old.reshape(8, 128),
            frac_trans.reshape(8, 128),
            frac_upwind.reshape(8, 128),
            frac_storage,
        ],
        "ssss" + "H" * 9,
        out_spaces="svvvv",
        scratch=[
            pltpu.VMEM((3, 1, 32, 128), jnp.int32),
            pltpu.VMEM((8, 128), jnp.int32),
            pltpu.VMEM((2, 1024), F32),
            pltpu.SemaphoreType.DMA((9,)),
        ],
        name="pack",
    )
    records = lax.all_gather(record, "frac", axis=0, tiled=True)
    one_right, one_left, records = after(one_right, one_left, records)
    below, above = ring(message, "region", 1), ring(message, "region", -1)
    half = blocks // 2
    two = [ring(one_right[:half], "frac", 2), ring(one_left[half:], "frac", -2)]
    same = [coupling, one_right, *two, one_left]
    pieces = same + [swapped(x, "frac") for x in same]
    room = 8 * blocks + UNROLL
    slots, rows, places, count, seg_old, seg_face, seg_up, seg_store, seg_live, left, right = call(
        survey,
        [
            smem_i32(room),
            smem_i32(room),
            smem_i32(room),
            smem_i32(1),
            vmem(128, 128),
            vmem(128, 128),
            vmem(128, 128),
            vmem(128, 128),
            vmem(8, 128),
            vmem(160, 128),
            vmem(160, 128),
        ],
        [ids, records],
        "Sv",
        out_spaces="ssss" + "v" * 7,
        scratch=[
            pltpu.VMEM((8, 128), jnp.int32),
            pltpu.SMEM((8, 128), jnp.int32),
            pltpu.SemaphoreType.DMA,
        ],
        name="survey",
    )
    around = [below, above, left, right]
    faces, own_up = call(
        geometry,
        [vmem(192, 128), vmem(192, 128)],
        [ids, message, *around, flag_y],
        "Svvvvvv",
        name="geometry",
    )
    [weights] = call(
        collect,
        [vmem(room, 64, 128)],
        [places, count, *pieces],
        "SS" + "a" * 10,
        scratch=[pltpu.SemaphoreType.DMA((room,))],
        name="collect",
    )
    lists = [slots, rows, count]
    store = storage.reshape(64, 128)
    wells = source.reshape(64, 128)
    inner = [vmem(128, 128), vmem(256, 128)]
    devices = lax.axis_size("region") * lax.axis_size("frac")

    cell, seg = cell_old, seg_old
    near = around
    parts = None
    for newton in range(NEWTON):
        args = [
            *lists,
            cell_old,
            store,
            wells,
            faces,
            own_up,
            seg_old,
            seg_store,
            seg_face,
            seg_up,
            seg_live,
            weights,
            cell,
            *near,
            seg,
        ]
        outs = [
            vmem(64, 128),
            vmem(128, 128),
            vmem(64, 128),
            vmem(128, 128),
            vmem(768, 128),
            vmem(512, 128),
            vmem(96, 128),
            vmem(192, 128),
            vmem(160, 128),
            vmem(128, 128),
            vmem(64, 128),
            vmem(room, 64, 128),
        ]
        if newton:
            args += [parts, *dir_cells, *dir_segs, *[x for group in dir_around for x in group]]
            outs += [vmem(64, 128), vmem(128, 128)]
        made = call(
            lambda *refs, newton=newton: linearise(newton, *refs),
            outs,
            args,
            "SSS" + "v" * (len(args) - 3),
            scratch=[*inner, vmem(32, 128), vmem(32, 128)],
            name="linearise",
        )
        base_cell, base_seg, dir_cell, dir_seg = made[:4]
        coef, seg_coef, lead, seg_lead, lines, reach, couple_rows, levels = made[4:12]
        if newton:
            cell, seg = made[12:]
        base_cells, base_segs = [base_cell], [base_seg]
        dir_cells, dir_segs, dir_around = [], [], []
        for sweep in range(SWEEPS):
            last = sweep == SWEEPS - 1
            nearby = exchanged(dir_cell)
            inflow, returned = call(
                couple_dirs,
                [vmem(128, 128), vmem(32, 128)],
                [*lists, dir_cell, dir_seg, lines, reach, weights, levels],
                "SSS" + "v" * 6,
                scratch=inner[:1],
                name="couple",
            )
            dir_cells.append(dir_cell)
            dir_segs.append(dir_seg)
            dir_around.append(nearby)
            args = [
                dir_cell,
                *nearby,
                dir_seg,
                inflow,
                returned,
                store,
                own_up,
                seg_store,
                seg_up,
                seg_live,
                coef,
                seg_coef,
                lead,
                seg_lead,
                lines,
                couple_rows,
            ]
            made = call(
                lambda *refs, last=last: advance(last, *refs),
                [vmem(64, 128), vmem(128, 128)] * (1 if last else 2),
                args,
                "v" * len(args),
                name="advance",
            )
            base_cells.append(made[0])
            base_segs.append(made[1])
            if not last:
                dir_cell, dir_seg = made[2:]
        [parts] = call(
            inner_products,
            [vmem(devices, 1, 128)],
            [*base_cells, *base_segs],
            "v" * (2 * SWEEPS + 2),
            name="inner_products",
        )
        parts = lax.all_to_all(parts, ("region", "frac"), 0, 0)

    args = [ids, parts, cell, seg, seg_old, *dir_cells, *dir_segs]
    cell_state, moved = call(
        finish,
        [jax.ShapeDtypeStruct((64, 128), F32), vmem(8, 16, 128)],
        args,
        "S" + "v" * (len(args) - 1),
        name="finish",
    )
    moved = jnp.sum(lax.all_to_all(moved, "frac", 0, 0), axis=0)
    seg_state = jnp.stack([frac_pres_old, frac_satur_old]) + moved.reshape(2, -1)
    return (cell_state.reshape(2, 1, 32, 128), seg_state)


def solution(mesh):
    placed = (
        P("region", None, "frac"),
        P("region", None, "frac"),
        P("region", None, "frac"),
        P(None, "region", None, "frac"),
        P(None, "region", None, "frac"),
        P(None, "region", None, "frac"),
        P(("region", "frac")),
        P(("region", "frac")),
        P(None, ("region", "frac")),
        P(("region", "frac")),
        P(("region", "frac")),
        P(("region", "frac"), None, None),
        P(("region", "frac")),
        P(("region", "frac")),
        P(("region", "frac")),
    )
    return jax.shard_map(
        on_device,
        mesh=mesh,
        in_specs=placed,
        out_specs=(P(None, "region", None, "frac"), P(None, ("region", "frac"))),
        check_vma=False,
    )
```

```python
import jax
import jax.numpy as jnp
from jax import lax
from jax.experimental import pallas as pl
from jax.experimental.pallas import tpu as pltpu
from jax.sharding import PartitionSpec as P

NEWTON = 2
SWEEPS = 5
VISCOSITY_RATIO = 0.5
TINY = 1e-06
SCALE = 1.0 / 16.0
UNROLL = 4
PAIRS = [(i, j) for i in range(SWEEPS + 1) for j in range(i, SWEEPS + 1)]
F32 = jnp.float32
VMEM_LIMIT = 24 * 2**20


def vmem(*shape):
    return pltpu.VMEM(shape, F32)


def smem_i32(*shape):
    return pltpu.SMEM(shape, jnp.int32)


def call(body, outs, args, spaces, scratch=(), out_spaces=None, flops=20000, name=None):
    ins = []
    for arg, space in zip(args, spaces):
        if space == "v":
            arg = pltpu.with_memory_space_constraint(arg, pltpu.VMEM)
        elif space == "H":
            arg = pltpu.with_memory_space_constraint(arg, pltpu.HBM)
        elif space == "S":
            arg = pltpu.with_memory_space_constraint(arg, pltpu.SMEM)
        ins.append(arg)
    kinds = {"v": pltpu.VMEM, "h": pltpu.VMEM, "s": pltpu.SMEM, "S": pltpu.SMEM, "a": pl.ANY, "H": pltpu.HBM}
    out_spaces = out_spaces or "v" * len(outs)
    return pl.pallas_call(
        body,
        out_shape=list(outs),
        in_specs=[pl.BlockSpec(memory_space=kinds[s]) for s in spaces],
        out_specs=[pl.BlockSpec(memory_space=kinds[s]) for s in out_spaces],
        scratch_shapes=list(scratch),
        compiler_params=pltpu.CompilerParams(vmem_limit_bytes=VMEM_LIMIT),
        cost_estimate=pl.CostEstimate(flops=flops, bytes_accessed=flops, transcendentals=0),
        name=name,
    )(*ins)


def mobility(satur):
    water_mob = satur * satur
    total_mob = water_mob + VISCOSITY_RATIO * (1.0 - satur) * (1.0 - satur)
    return water_mob, total_mob


def slopes(satur):
    return 2.0 * satur, 2.0 * satur - 2.0 * VISCOSITY_RATIO * (1.0 - satur)


def neighbours(own, below, above, left, right):
    lane = lax.broadcasted_iota(jnp.int32, own.shape, 1)
    x_next = jnp.where(lane == 127, pltpu.roll(right, 127, 1), pltpu.roll(own, 127, 1))
    x_prev = jnp.where(lane == 0, pltpu.roll(left, 1, 1), pltpu.roll(own, 1, 1))
    return (above, below, pltpu.roll(own, 31, 0), pltpu.roll(own, 1, 0), x_next, x_prev)


def chain_neighbours(own):
    return (pltpu.roll(own, 63, 0), pltpu.roll(own, 1, 0))


def harmonic(left_val, right_val):
    return 2.0 * left_val * right_val / (left_val + right_val)


def geometry(ids, own, below, above, left, right, flag_y, faces_ref, own_up_ref):
    region, frac, regions, fracs = ids[0], ids[1], ids[2], ids[3]
    block = [r[...] for r in (own, below, above, left, right)]
    perm = neighbours(*[b[64:96] for b in block])
    row = lax.broadcasted_iota(jnp.int32, (32, 128), 0)
    lane = lax.broadcasted_iota(jnp.int32, (32, 128), 1)
    everywhere = row >= 0
    inside = (
        everywhere & (region < regions - 1),
        everywhere & (region > 0),
        row < 31,
        row > 0,
        (lane < 127) | (frac < fracs - 1),
        (lane > 0) | (frac > 0),
    )
    here = block[0][64:96]
    for f in range(6):
        faces_ref[32 * f : 32 * f + 32] = jnp.where(inside[f], harmonic(here, perm[f]), 0.0)
    flag_z = block[0][96:128]
    flag_x = block[0][128:160]
    y_here = flag_y[...]
    z_prev = block[1][96:128]
    y_prev = pltpu.roll(y_here, 1, 0)
    x_prev = neighbours(flag_x, flag_x, flag_x, block[3][128:160], flag_x)[5]
    for f, (flag, forward) in enumerate(
        ((flag_z, 1), (z_prev, 0), (y_here, 1), (y_prev, 0), (flag_x, 1), (x_prev, 0))
    ):
        upstream = jnp.where(flag == 1.0, 1.0, 0.0)
        own_up_ref[32 * f : 32 * f + 32] = upstream if forward else 1.0 - upstream


def pack(
    ids, parts, rows, live, pres, satur, perm, flags, q, r, trans, ups, store,
    ids_out, message, records, cell, flag_y, record, flag_room, up_room, store_room, sems,
):
    copies = [
        pltpu.make_async_copy(src, dst, sems.at[n])
        for n, (src, dst) in enumerate(
            (
                (pres.at[0], cell.at[0:32]),
                (satur.at[0], cell.at[32:64]),
                (perm.at[0], message.at[64:96]),
                (flags, flag_room),
                (q, record.at[0:8]),
                (r, record.at[8:16]),
                (trans, record.at[16:24]),
                (ups, up_room),
                (store, store_room),
            )
        )
    ]
    for copy in copies:
        copy.start()
    for k in range(4):
        ids_out[k] = ids[k]
    lane = lax.broadcasted_iota(jnp.int32, (8, 128), 1)
    codes = jnp.full((8, 128), -1.0, F32)
    for k in range(16):
        code = jnp.where(k < live[0], parts[k] * 32 + rows[k], -1)
        codes = jnp.where(lane == k, code.astype(F32), codes)
    record[48:56] = codes
    for copy in copies:
        copy.wait()
    message[0:64] = cell[...]
    message[96:128] = flag_room[0, 0].astype(F32)
    message[128:160] = flag_room[2, 0].astype(F32)
    flag_y[...] = flag_room[1, 0].astype(F32)
    record[24:32] = up_room[...].astype(F32)
    for k in range(8):
        for c in range(2):
            row = 32 + 8 * c + k
            record[row : row + 1] = store_room[c : c + 1, 128 * k : 128 * k + 128]
    first = message[0:128].T
    rest = jnp.concatenate([message[128:160], jnp.zeros((96, 128), F32)], axis=0).T
    record[49:50] = first[127:128]
    record[50:51] = rest[127:128]
    record[51:52] = first[0:1]
    record[52:53] = rest[0:1]
    copied = record[...]
    for k in range(8):
        records[k] = copied


def owner_of(piece, me):
    base = me if piece < 4 else me + 1 - 2 * (me & 1)
    return (base - 2 * (piece % 4) + 8) & 7


def halves(first, second):
    low = lax.broadcasted_iota(jnp.int32, first.shape, 1) < 64
    return (
        jnp.where(low, first, pltpu.roll(second, 64, 1)),
        jnp.where(low, pltpu.roll(first, 64, 1), second),
    )


def survey(
    ids, records,
    slots, rows, places, count, seg_old, seg_face, seg_up, seg_store, seg_live, left, right,
    code_room, codes, sem,
):
    me = ids[1]
    lane = lax.broadcasted_iota(jnp.int32, (8, 128), 1)
    places_of = [pl.multiple_of(owner_of(k, me) * 56, 8) for k in range(8)]
    for k in range(8):
        code_room[k : k + 1] = records[pl.ds(places_of[k] + 48, 8), :][:1].astype(jnp.int32)
    copy = pltpu.make_async_copy(code_room, codes, sem)
    copy.start()

    for side, owner, row in ((left, (me + 7) & 7, 1), (right, (me + 1) & 7, 3)):
        columns = records[pl.ds(pl.multiple_of(owner * 56, 8) + 48, 8), :]
        side[0:128] = jnp.broadcast_to(columns[row : row + 1], (128, 128)).T
        side[128:160] = jnp.broadcast_to(columns[row + 1 : row + 2], (128, 128)).T[:32]

    copy.wait()

    def visit(slot, carry):
        n, live = carry
        for k in range(8):
            code = codes[k, slot]
            mine = (code >> 5) == me
            place = (slot & 1) * 64 + 8 * k + (slot >> 1)
            slots[n] = place
            rows[n] = code & 31
            places[n] = 16 * k + slot
            live = jnp.where(lane == jnp.where(mine, place, -1), 1.0, live)
            n = n + jnp.where(mine, 1, 0)
        return n, live

    n, live = lax.fori_loop(0, 16, visit, (jnp.int32(0), jnp.zeros((8, 128), F32)))
    seg_live[...] = live
    count[0] = (n + UNROLL - 1) // UNROLL
    for k in range(UNROLL - 1):
        slots[n + k] = -1
        rows[n + k] = 0
        places[n + k] = 0

    def field(k):
        return jnp.concatenate([records[pl.ds(p + 8 * k, 8), :] for p in places_of], axis=0)

    def turned(k):
        both = jnp.concatenate([field(k), field(k + 1)], axis=0).T
        return halves(both[:64], both[64:])

    seg_old[:64], seg_old[64:] = turned(0)
    trans, flags = turned(2)
    at = lax.broadcasted_iota(jnp.int32, (64, 128), 0)
    seg_face[:64] = jnp.where(at < 63, trans, 0.0)
    seg_face[64:] = jnp.where(at > 0, pltpu.roll(trans, 1, 0), 0.0)
    upstream = jnp.where(flags == 1.0, 1.0, 0.0)
    seg_up[:64] = upstream
    seg_up[64:] = 1.0 - pltpu.roll(upstream, 1, 0)
    seg_store[:64], seg_store[64:] = turned(4)


def collect(places, count, *refs):
    pieces, weights, sems = refs[:10], refs[10], refs[11]
    starts = (0, 16, 32, 40, 48, 64, 80, 96, 104, 112, 128)

    def fetch(i, carry):
        place = places[i]
        for k in range(10):

            @pl.when((place >= starts[k]) & (place < starts[k + 1]))
            def _():
                pltpu.make_async_copy(pieces[k].at[place - starts[k]], weights.at[i], sems.at[i]).start()

        return carry

    def settle(i, carry):
        pltpu.make_async_copy(pieces[0].at[0], weights.at[i], sems.at[i]).wait()
        return carry

    lax.fori_loop(0, count[0] * UNROLL, fetch, 0)
    lax.fori_loop(0, count[0] * UNROLL, settle, 0)


def survey_blocks(slots, rows, count, weights, lines, q, sums, returned, columns, levels):
    lane = lax.broadcasted_iota(jnp.int32, (64, 128), 1)
    sums[...] = jnp.zeros_like(sums)
    returned[...] = jnp.zeros_like(returned)
    columns[...] = jnp.zeros_like(columns)

    def body(step, carry):
        added = [jnp.zeros((64, 128), F32) for _ in range(4)]
        q_all = q[:64]
        backs = []
        for k in range(UNROLL):
            i = step * UNROLL + k
            slot, row = slots[i], rows[i]
            weight = weights[i]
            here = lane == slot
            for v in range(4):
                line = lines[pl.ds(32 * v + row, 1), :]
                total = jnp.sum(weight * line, axis=1, keepdims=True)
                added[v] = added[v] + jnp.where(here, total, 0.0)
            q_col = jnp.sum(jnp.where(here, q_all, 0.0), axis=1, keepdims=True)
            levels[i] = jnp.broadcast_to(q_col, (64, 128))
            back = jnp.sum(weight * q_col, axis=0, keepdims=True)
            valid = jnp.where(slot >= 0, 1.0, 0.0)
            backs.append((row, back, jnp.sum(weight, axis=0, keepdims=True) * valid))
        for v in range(4):
            sums[64 * v : 64 * v + 64] += added[v]
        for row, back, col in backs:
            returned[pl.ds(row, 1), :] += back
            columns[pl.ds(row, 1), :] += col
        return carry

    lax.fori_loop(0, count[0], body, 0)


def couple_blocks(slots, rows, count, weights, levels, lines, dq, inflow, returned):
    lane = lax.broadcasted_iota(jnp.int32, (64, 128), 1)
    returned[...] = jnp.zeros_like(returned)

    def body(step, carry):
        added = [jnp.zeros((64, 128), F32) for _ in range(2)]
        dq_all = dq[:64]
        backs = []
        for k in range(UNROLL):
            i = step * UNROLL + k
            slot, row = slots[i], rows[i]
            weight, level = weights[i], levels[i]
            here = lane == slot
            for v in range(2):
                first = lines[pl.ds(32 * v + row, 1), :]
                second = lines[pl.ds(64 + 32 * v + row, 1), :]
                total = jnp.sum(weight * (first - level * second), axis=1, keepdims=True)
                added[v] = added[v] + jnp.where(here, total, 0.0)
            dq_col = jnp.sum(jnp.where(here, dq_all, 0.0), axis=1, keepdims=True)
            backs.append((row, jnp.sum(weight * dq_col, axis=0, keepdims=True)))
        for v in range(2):
            inflow[64 * v : 64 * v + 64] += added[v]
        for row, back in backs:
            returned[pl.ds(row, 1), :] += back
        return carry

    lax.fori_loop(0, count[0], body, 0)


def combine(dots):
    total = jnp.broadcast_to(dots, (128, 128)).T
    gram = {}
    for n, (i, j) in enumerate(PAIRS):
        gram[i, j] = gram[j, i] = jnp.broadcast_to(total[n : n + 1, :], (8, 128))
    one = jnp.ones((8, 128), F32)
    remain = [one]
    factors = [jnp.zeros((8, 128), F32) for _ in range(SWEEPS)]
    for sweep in range(SWEEPS):
        image = [(j + 1, value / SCALE) for j, value in enumerate(remain)]
        cross = sum(value * factor * gram[j, i] for j, value in enumerate(remain) for i, factor in image)
        square = sum(a * b * gram[i, j] for i, a in image for j, b in image)
        alpha = cross / (square + TINY)
        for j, value in enumerate(remain):
            factors[j] = factors[j] + alpha * value
        longer = remain + [jnp.zeros((8, 128), F32)]
        for i, factor in image:
            longer[i] = longer[i] - alpha * factor
        remain = longer
    return factors


def spread(factor, rows):
    return jnp.broadcast_to(factor[:1], (rows, 128))


def summed(parts_ref):
    return jnp.sum(parts_ref[...], axis=0)


def face_terms(pres, satur, pres_across, satur_across, faces, own_up, coef_ref, stride):
    div_t = div_w = diag_t = diag_w = None
    count = len(pres_across)
    rows = pres.shape[0]
    for f in range(count):
        trans = faces[rows * f : rows * f + rows]
        up = own_up[rows * f : rows * f + rows]
        s_up = jnp.where(up == 1.0, satur, satur_across[f])
        drop = pres - pres_across[f]
        water, total = mobility(s_up)
        water_slope, total_slope = slopes(s_up)
        cond_t, cond_w = trans * total, trans * water
        lean = trans * drop
        at = rows * f
        coef_ref[at : at + rows] = cond_t
        coef_ref[stride + at : stride + at + rows] = cond_w
        coef_ref[2 * stride + at : 2 * stride + at + rows] = total_slope * lean
        coef_ref[3 * stride + at : 3 * stride + at + rows] = water_slope * lean
        flux_t, flux_w = cond_t * drop, cond_w * drop
        if f == 0:
            div_t, div_w, diag_t, diag_w = flux_t, flux_w, cond_t, cond_w
        else:
            div_t, div_w = div_t + flux_t, div_w + flux_w
            diag_t, diag_w = diag_t + cond_t, diag_w + cond_w
    return div_t, div_w, diag_t, diag_w


def face_tangents(dp, ds, dp_across, ds_across, own_up, coef, stride):
    rows = dp.shape[0]
    out_t = out_w = None
    for f in range(len(dp_across)):
        at = rows * f
        up = own_up[at : at + rows]
        drop = dp - dp_across[f]
        ds_up = jnp.where(up == 1.0, ds, ds_across[f])
        part_t = coef[at : at + rows] * drop + coef[2 * stride + at : 2 * stride + at + rows] * ds_up
        part_w = (
            coef[stride + at : stride + at + rows] * drop
            + coef[3 * stride + at : 3 * stride + at + rows] * ds_up
        )
        out_t = part_t if f == 0 else out_t + part_t
        out_w = part_w if f == 0 else out_w + part_w
    return out_t, out_w


def linearise(newton, *refs):
    refs = list(refs)

    def take(n):
        out = refs[:n]
        del refs[:n]
        return out

    slots, rows, count = take(3)
    cell_old, store, source, faces, own_up = take(5)
    seg_old, seg_store, seg_face, seg_up, seg_live, weights = take(6)
    [cell_in] = take(1)
    around = take(4)
    [seg_in] = take(1)
    if newton:
        [parts] = take(1)
        dir_cells = take(SWEEPS)
        dir_segs = take(SWEEPS)
        dir_around = [take(4) for _ in range(SWEEPS)]
    base_cell, base_seg, dir_cell, dir_seg = take(4)
    coef, seg_coef, lead, seg_lead, lines, reach, couple_rows, levels = take(8)
    if newton:
        cell_out, seg_out = take(2)
    inner_lines, sums, returned, columns = refs

    cell = cell_in[...]
    near = [r[0:64] for r in around]
    if newton:
        factors = combine(summed(parts))
        for j in range(SWEEPS):
            g = spread(factors[j], 64)
            cell = cell + g * dir_cells[j][...]
            near = [n + g * d[...] for n, d in zip(near, dir_around[j])]
        cell_out[...] = cell
        seg = seg_in[...]
        for j in range(SWEEPS):
            seg = seg + spread(factors[j], 128) * dir_segs[j][...]
        seg_out[...] = seg
        seg_ref = seg_out
    else:
        seg = seg_in[...]
        seg_ref = seg_in
    pres, satur = cell[:32], cell[32:]
    q, r = seg[:64], seg[64:]

    water, total = mobility(satur)
    water_slope, total_slope = slopes(satur)
    lines[0:32] = total
    lines[32:64] = water
    lines[64:96] = total_slope
    lines[96:128] = water_slope
    lines[128:160] = pres
    inner_lines[0:32] = total
    inner_lines[32:64] = water
    inner_lines[64:96] = total * pres
    inner_lines[96:128] = water * pres
    survey_blocks(slots, rows, count, weights, inner_lines, seg_ref, sums, returned, columns, levels)
    reach[...] = sums[0:128]
    column = columns[...]
    pull = pres * column - returned[...]
    couple_rows[0:32] = column
    couple_rows[32:64] = pull

    pres_across = neighbours(pres, *[n[:32] for n in near])
    satur_across = neighbours(satur, *[n[32:] for n in near])
    div_t, div_w, diag_t, diag_w = face_terms(
        pres, satur, pres_across, satur_across, faces, own_up, coef, 192
    )
    st, sw = store[:32], store[32:]
    moved = cell - cell_old[...]
    base_t = source[:32] - st * moved[:32] - div_t - total * pull
    base_w = source[32:] - sw * moved[32:] - div_w - water * pull
    lead_t = 1.0 / (st + diag_t)
    lead_w = 1.0 / sw
    lead[0:32] = lead_t
    lead[32:64] = diag_w
    lead[64:96] = lead_w
    base_cell[0:32] = base_t
    base_cell[32:64] = base_w
    first = base_t * lead_t
    dir_cell[0:32] = first
    dir_cell[32:64] = (base_w - diag_w * first) * lead_w

    chain_t, chain_w, chain_dt, chain_dw = face_terms(
        q, r, chain_neighbours(q), chain_neighbours(r), seg_face, seg_up, seg_coef, 128
    )
    live = jnp.broadcast_to(seg_live[:1], (64, 128))
    sst, ssw = seg_store[:64], seg_store[64:]
    shifted = seg - seg_old[...]
    inflow_t = sums[128:192] - q * sums[0:64]
    inflow_w = sums[192:256] - q * sums[64:128]
    seg_t = -live * (sst * shifted[:64] + chain_t - inflow_t)
    seg_w = -live * (ssw * shifted[64:] + chain_w - inflow_w)
    lead_t = 1.0 / (sst + chain_dt)
    lead_w = 1.0 / ssw
    seg_lead[0:64] = lead_t
    seg_lead[64:128] = chain_dw
    seg_lead[128:192] = lead_w
    base_seg[0:64] = seg_t
    base_seg[64:128] = seg_w
    first = seg_t * lead_t
    dir_seg[0:64] = first
    dir_seg[64:128] = (seg_w - chain_dw * first) * lead_w


def couple_dirs(
    slots, rows, count, dir_cell, dir_seg, lines, reach, weights, levels, inflow, returned, inner_lines
):
    dp, ds = dir_cell[:32], dir_cell[32:]
    pres = lines[128:160]
    lean_t = lines[64:96] * ds
    lean_w = lines[96:128] * ds
    inner_lines[0:32] = lines[0:32] * dp + lean_t * pres
    inner_lines[32:64] = lines[32:64] * dp + lean_w * pres
    inner_lines[64:96] = lean_t
    inner_lines[96:128] = lean_w
    dq = dir_seg[:64]
    inflow[0:64] = -dq * reach[0:64]
    inflow[64:128] = -dq * reach[64:128]
    couple_blocks(slots, rows, count, weights, levels, inner_lines, dir_seg, inflow, returned)


def advance(last, *refs):
    (
        dir_cell,
        below,
        above,
        left,
        right,
        dir_seg,
        inflow,
        returned,
        store,
        own_up,
        seg_store,
        seg_up,
        seg_live,
        coef,
        seg_coef,
        lead,
        seg_lead,
        lines,
        couple_rows,
    ) = refs[:19]
    next_cell, next_seg = refs[19:21]
    dp, ds = dir_cell[:32], dir_cell[32:]
    near = [n[...] for n in (below, above, left, right)]
    out_t, out_w = face_tangents(
        dp,
        ds,
        neighbours(dp, *[n[:32] for n in near]),
        neighbours(ds, *[n[32:] for n in near]),
        own_up,
        coef,
        192,
    )
    flow = dp * couple_rows[0:32] - returned[...]
    pull = ds * couple_rows[32:64]
    image_t = store[:32] * dp + out_t + lines[0:32] * flow + lines[64:96] * pull
    image_w = store[32:] * ds + out_w + lines[32:64] * flow + lines[96:128] * pull
    cell_t, cell_w = SCALE * image_t, SCALE * image_w
    next_cell[0:32] = cell_t
    next_cell[32:64] = cell_w

    dq, dr = dir_seg[:64], dir_seg[64:]
    chain_t, chain_w = face_tangents(
        dq, dr, chain_neighbours(dq), chain_neighbours(dr), seg_up, seg_coef, 128
    )
    live = jnp.broadcast_to(SCALE * seg_live[:1], (64, 128))
    seg_t = live * (seg_store[:64] * dq + chain_t - inflow[:64])
    seg_w = live * (seg_store[64:] * dr + chain_w - inflow[64:])
    next_seg[0:64] = seg_t
    next_seg[64:128] = seg_w
    if not last:
        next_dir, next_dir_seg = refs[21:23]
        first = cell_t * lead[0:32]
        next_dir[0:32] = first
        next_dir[32:64] = (cell_w - lead[32:64] * first) * lead[64:96]
        first = seg_t * seg_lead[0:64]
        next_dir_seg[0:64] = first
        next_dir_seg[64:128] = (seg_w - seg_lead[64:128] * first) * seg_lead[128:192]


def inner_products(*refs):
    cells, segs, out = refs[: SWEEPS + 1], refs[SWEEPS + 1 : 2 * SWEEPS + 2], refs[-1]
    lines = []
    for i, j in PAIRS:
        part = jnp.sum(cells[i][...] * cells[j][...], axis=0, keepdims=True)
        lines.append(part + jnp.sum(segs[i][...] * segs[j][...], axis=0, keepdims=True))
    lines.append(jnp.zeros((128 - len(PAIRS), 128), F32))
    total = jnp.sum(jnp.concatenate(lines, axis=0).T, axis=0, keepdims=True)
    out[...] = jnp.broadcast_to(total[None], out.shape)


def finish(*refs):
    ids, parts, cell, seg, seg_old = refs[:5]
    dir_cells = refs[5 : 5 + SWEEPS]
    dir_segs = refs[5 + SWEEPS : 5 + 2 * SWEEPS]
    cell_out, moved = refs[5 + 2 * SWEEPS :]
    factors = combine(summed(parts))
    total = cell[...]
    shift = seg[...] - seg_old[...]
    for j in range(SWEEPS):
        total = total + spread(factors[j], 64) * dir_cells[j][...]
        shift = shift + spread(factors[j], 128) * dir_segs[j][...]
    cell_out[...] = total
    turned = jnp.concatenate(halves(shift[:64], shift[64:]), axis=0).T
    me = ids[1]
    for k in range(8):
        owner = owner_of(k, me)
        moved[owner, 0:8] = turned[8 * k : 8 * k + 8]
        moved[owner, 8:16] = turned[64 + 8 * k : 64 + 8 * k + 8]


def ring(block, axis, distance):
    count = lax.axis_size(axis)
    return lax.ppermute(block, axis, [(i, (i + distance) % count) for i in range(count)])


def swapped(block, axis):
    return lax.ppermute(block, axis, [(i, i ^ 1) for i in range(lax.axis_size(axis))])


def exchanged(block):
    left, right = ring(block, "frac", 1), ring(block, "frac", -1)
    return [ring(block, "region", 1), ring(block, "region", -1), left, right]


def after(first, *others):
    return lax.optimization_barrier((first, *others))


def on_device(
    pres_old,
    satur_old,
    permeability,
    storage,
    source,
    face_upwind,
    frac_pres_old,
    frac_satur_old,
    frac_storage,
    frac_trans,
    frac_upwind,
    coupling,
    target_part,
    target_row,
    live_count,
):
    blocks = coupling.shape[0]
    ids = jnp.stack(
        [
            lax.axis_index("region"),
            lax.axis_index("frac"),
            jnp.int32(lax.axis_size("region")),
            jnp.int32(lax.axis_size("frac")),
        ]
    ).astype(jnp.int32)
    one_right = ring(coupling, "frac", 2)
    one_left = ring(coupling, "frac", -2)
    ids, message, record, cell_old, flag_y = call(
        pack,
        [smem_i32(4), vmem(160, 128), vmem(8, 56, 128), vmem(64, 128), vmem(32, 128)],
        [
            ids,
            target_part,
            target_row,
            live_count,
            pres_old,
            satur_old,
            permeability,
            face_upwind,
            frac_pres_old.reshape(8, 128),
            frac_satur_old.reshape(8, 128),
            frac_trans.reshape(8, 128),
            frac_upwind.reshape(8, 128),
            frac_storage,
        ],
        "ssss" + "H" * 9,
        out_spaces="svvvv",
        scratch=[
            vmem(56, 128),
            pltpu.VMEM((3, 1, 32, 128), jnp.int32),
            pltpu.VMEM((8, 128), jnp.int32),
            pltpu.VMEM((2, 1024), F32),
            pltpu.SemaphoreType.DMA((9,)),
        ],
        name="pack",
    )
    records = lax.all_to_all(record, "frac", 0, 0).reshape(448, 128)
    one_right, one_left, records = after(one_right, one_left, records)
    below, above = ring(message, "region", 1), ring(message, "region", -1)
    half = blocks // 2
    two = [ring(one_right[:half], "frac", 2), ring(one_left[half:], "frac", -2)]
    same = [coupling, one_right, *two, one_left]
    pieces = same + [swapped(x, "frac") for x in same]
    room = 8 * blocks + UNROLL
    slots, rows, places, count, seg_old, seg_face, seg_up, seg_store, seg_live, left, right = call(
        survey,
        [
            smem_i32(room),
            smem_i32(room),
            smem_i32(room),
            smem_i32(1),
            vmem(128, 128),
            vmem(128, 128),
            vmem(128, 128),
            vmem(128, 128),
            vmem(8, 128),
            vmem(160, 128),
            vmem(160, 128),
        ],
        [ids, records],
        "Sv",
        out_spaces="ssss" + "v" * 7,
        scratch=[
            pltpu.VMEM((8, 128), jnp.int32),
            pltpu.SMEM((8, 128), jnp.int32),
            pltpu.SemaphoreType.DMA,
        ],
        flops=6_000_000,
        name="survey",
    )
    around = [below, above, left, right]
    faces, own_up = call(
        geometry,
        [vmem(192, 128), vmem(192, 128)],
        [ids, message, *around, flag_y],
        "Svvvvvv",
        flops=2_000_000,
        name="geometry",
    )
    [weights] = call(
        collect,
        [vmem(room, 64, 128)],
        [places, count, *pieces],
        "SSH" + "a" * 9,
        scratch=[pltpu.SemaphoreType.DMA((room,))],
        name="collect",
    )
    lists = [slots, rows, count]
    store = storage.reshape(64, 128)
    wells = source.reshape(64, 128)
    inner = [vmem(128, 128), vmem(256, 128)]
    devices = lax.axis_size("region") * lax.axis_size("frac")

    cell, seg = cell_old, seg_old
    near = around
    parts = None
    for newton in range(NEWTON):
        args = [
            *lists,
            cell_old,
            store,
            wells,
            faces,
            own_up,
            seg_old,
            seg_store,
            seg_face,
            seg_up,
            seg_live,
            weights,
            cell,
            *near,
            seg,
        ]
        outs = [
            vmem(64, 128),
            vmem(128, 128),
            vmem(64, 128),
            vmem(128, 128),
            vmem(768, 128),
            vmem(512, 128),
            vmem(96, 128),
            vmem(192, 128),
            vmem(160, 128),
            vmem(128, 128),
            vmem(64, 128),
            vmem(room, 64, 128),
        ]
        if newton:
            args += [parts, *dir_cells, *dir_segs, *[x for group in dir_around for x in group]]
            outs += [vmem(64, 128), vmem(128, 128)]
        made = call(
            lambda *refs, newton=newton: linearise(newton, *refs),
            outs,
            args,
            "SSS" + "v" * (len(args) - 3),
            scratch=[*inner, vmem(32, 128), vmem(32, 128)],
            name="linearise",
        )
        base_cell, base_seg, dir_cell, dir_seg = made[:4]
        coef, seg_coef, lead, seg_lead, lines, reach, couple_rows, levels = made[4:12]
        if newton:
            cell, seg = made[12:]
        base_cells, base_segs = [base_cell], [base_seg]
        dir_cells, dir_segs, dir_around = [], [], []
        for sweep in range(SWEEPS):
            last = sweep == SWEEPS - 1
            nearby = exchanged(dir_cell)
            inflow, returned = call(
                couple_dirs,
                [vmem(128, 128), vmem(32, 128)],
                [*lists, dir_cell, dir_seg, lines, reach, weights, levels],
                "SSS" + "v" * 6,
                scratch=inner[:1],
                name="couple",
            )
            dir_cells.append(dir_cell)
            dir_segs.append(dir_seg)
            dir_around.append(nearby)
            args = [
                dir_cell,
                *nearby,
                dir_seg,
                inflow,
                returned,
                store,
                own_up,
                seg_store,
                seg_up,
                seg_live,
                coef,
                seg_coef,
                lead,
                seg_lead,
                lines,
                couple_rows,
            ]
            made = call(
                lambda *refs, last=last: advance(last, *refs),
                [vmem(64, 128), vmem(128, 128)] * (1 if last else 2),
                args,
                "v" * len(args),
                name="advance",
            )
            base_cells.append(made[0])
            base_segs.append(made[1])
            if not last:
                dir_cell, dir_seg = made[2:]
        [parts] = call(
            inner_products,
            [vmem(devices, 1, 128)],
            [*base_cells, *base_segs],
            "v" * (2 * SWEEPS + 2),
            name="inner_products",
        )
        parts = lax.all_to_all(parts, ("region", "frac"), 0, 0)

    args = [ids, parts, cell, seg, seg_old, *dir_cells, *dir_segs]
    cell_state, moved = call(
        finish,
        [jax.ShapeDtypeStruct((64, 128), F32), vmem(8, 16, 128)],
        args,
        "S" + "v" * (len(args) - 1),
        name="finish",
    )
    moved = jnp.sum(lax.all_to_all(moved, "frac", 0, 0), axis=0)
    seg_state = jnp.stack([frac_pres_old, frac_satur_old]) + moved.reshape(2, -1)
    return (cell_state.reshape(2, 1, 32, 128), seg_state)


def solution(mesh):
    placed = (
        P("region", None, "frac"),
        P("region", None, "frac"),
        P("region", None, "frac"),
        P(None, "region", None, "frac"),
        P(None, "region", None, "frac"),
        P(None, "region", None, "frac"),
        P(("region", "frac")),
        P(("region", "frac")),
        P(None, ("region", "frac")),
        P(("region", "frac")),
        P(("region", "frac")),
        P(("region", "frac"), None, None),
        P(("region", "frac")),
        P(("region", "frac")),
        P(("region", "frac")),
    )
    return jax.shard_map(
        on_device,
        mesh=mesh,
        in_specs=placed,
        out_specs=(P(None, "region", None, "frac"), P(None, ("region", "frac"))),
        check_vma=False,
    )
```

```python
import jax
import jax.numpy as jnp
from jax import lax
from jax.experimental import pallas as pl
from jax.experimental.pallas import tpu as pltpu
from jax.sharding import PartitionSpec as P

NEWTON = 2
SWEEPS = 5
VISCOSITY_RATIO = 0.5
TINY = 1e-06
SCALE = 1.0 / 16.0
UNROLL = 4
PAIRS = [(i, j) for i in range(SWEEPS + 1) for j in range(i, SWEEPS + 1)]
F32 = jnp.float32
VMEM_LIMIT = 24 * 2**20


def vmem(*shape):
    return pltpu.VMEM(shape, F32)


def smem_i32(*shape):
    return pltpu.SMEM(shape, jnp.int32)


def call(body, outs, args, spaces, scratch=(), out_spaces=None, flops=20000, name=None):
    ins = []
    for arg, space in zip(args, spaces):
        if space == "v":
            arg = pltpu.with_memory_space_constraint(arg, pltpu.VMEM)
        elif space == "H":
            arg = pltpu.with_memory_space_constraint(arg, pltpu.HBM)
        elif space == "S":
            arg = pltpu.with_memory_space_constraint(arg, pltpu.SMEM)
        ins.append(arg)
    kinds = {"v": pltpu.VMEM, "h": pltpu.VMEM, "s": pltpu.SMEM, "S": pltpu.SMEM, "a": pl.ANY, "H": pltpu.HBM}
    out_spaces = out_spaces or "v" * len(outs)
    return pl.pallas_call(
        body,
        out_shape=list(outs),
        in_specs=[pl.BlockSpec(memory_space=kinds[s]) for s in spaces],
        out_specs=[pl.BlockSpec(memory_space=kinds[s]) for s in out_spaces],
        scratch_shapes=list(scratch),
        compiler_params=pltpu.CompilerParams(vmem_limit_bytes=VMEM_LIMIT),
        cost_estimate=pl.CostEstimate(flops=flops, bytes_accessed=flops, transcendentals=0),
        name=name,
    )(*ins)


def mobility(satur):
    water_mob = satur * satur
    total_mob = water_mob + VISCOSITY_RATIO * (1.0 - satur) * (1.0 - satur)
    return water_mob, total_mob


def slopes(satur):
    return 2.0 * satur, 2.0 * satur - 2.0 * VISCOSITY_RATIO * (1.0 - satur)


def neighbours(own, below, above, left, right):
    lane = lax.broadcasted_iota(jnp.int32, own.shape, 1)
    x_next = jnp.where(lane == 127, pltpu.roll(right, 127, 1), pltpu.roll(own, 127, 1))
    x_prev = jnp.where(lane == 0, pltpu.roll(left, 1, 1), pltpu.roll(own, 1, 1))
    return (above, below, pltpu.roll(own, 31, 0), pltpu.roll(own, 1, 0), x_next, x_prev)


def chain_neighbours(own):
    return (pltpu.roll(own, 63, 0), pltpu.roll(own, 1, 0))


def harmonic(left_val, right_val):
    return 2.0 * left_val * right_val / (left_val + right_val)


def geometry(ids, own, below, above, left, right, flag_y, faces_ref, own_up_ref):
    region, frac, regions, fracs = ids[0], ids[1], ids[2], ids[3]
    block = [r[...] for r in (own, below, above, left, right)]
    perm = neighbours(*[b[64:96] for b in block])
    row = lax.broadcasted_iota(jnp.int32, (32, 128), 0)
    lane = lax.broadcasted_iota(jnp.int32, (32, 128), 1)
    everywhere = row >= 0
    inside = (
        everywhere & (region < regions - 1),
        everywhere & (region > 0),
        row < 31,
        row > 0,
        (lane < 127) | (frac < fracs - 1),
        (lane > 0) | (frac > 0),
    )
    here = block[0][64:96]
    for f in range(6):
        faces_ref[32 * f : 32 * f + 32] = jnp.where(inside[f], harmonic(here, perm[f]), 0.0)
    flag_z = block[0][96:128]
    flag_x = block[0][128:160]
    y_here = flag_y[...]
    z_prev = block[1][96:128]
    y_prev = pltpu.roll(y_here, 1, 0)
    x_prev = neighbours(flag_x, flag_x, flag_x, block[3][128:160], flag_x)[5]
    for f, (flag, forward) in enumerate(
        ((flag_z, 1), (z_prev, 0), (y_here, 1), (y_prev, 0), (flag_x, 1), (x_prev, 0))
    ):
        upstream = jnp.where(flag == 1.0, 1.0, 0.0)
        own_up_ref[32 * f : 32 * f + 32] = upstream if forward else 1.0 - upstream


def pack(
    ids, parts, rows, live, pres, satur, perm, flags, q, r, trans, ups, store,
    ids_out, message, records, cell, flag_y, record, flag_room, up_room, store_room, sems,
):
    copies = [
        pltpu.make_async_copy(src, dst, sems.at[n])
        for n, (src, dst) in enumerate(
            (
                (pres.at[0], cell.at[0:32]),
                (satur.at[0], cell.at[32:64]),
                (perm.at[0], message.at[64:96]),
                (flags, flag_room),
                (q, record.at[0:8]),
                (r, record.at[8:16]),
                (trans, record.at[16:24]),
                (ups, up_room),
                (store, store_room),
            )
        )
    ]
    for copy in copies:
        copy.start()
    for k in range(4):
        ids_out[k] = ids[k]
    lane = lax.broadcasted_iota(jnp.int32, (8, 128), 1)
    codes = jnp.full((8, 128), -1.0, F32)
    for k in range(16):
        code = jnp.where(k < live[0], parts[k] * 32 + rows[k], -1)
        codes = jnp.where(lane == k, code.astype(F32), codes)
    record[48:56] = codes
    for copy in copies:
        copy.wait()
    message[0:64] = cell[...]
    message[96:128] = flag_room[0, 0].astype(F32)
    message[128:160] = flag_room[2, 0].astype(F32)
    flag_y[...] = flag_room[1, 0].astype(F32)
    record[24:32] = up_room[...].astype(F32)
    for k in range(8):
        for c in range(2):
            row = 32 + 8 * c + k
            record[row : row + 1] = store_room[c : c + 1, 128 * k : 128 * k + 128]
    first = message[0:128].T
    rest = jnp.concatenate([message[128:160], jnp.zeros((96, 128), F32)], axis=0).T
    record[49:50] = first[127:128]
    record[50:51] = rest[127:128]
    record[51:52] = first[0:1]
    record[52:53] = rest[0:1]
    copied = record[...]
    for k in range(8):
        records[k] = copied


def owner_of(piece, me):
    base = me if piece < 4 else me + 1 - 2 * (me & 1)
    return (base - 2 * (piece % 4) + 8) & 7


def halves(first, second):
    low = lax.broadcasted_iota(jnp.int32, first.shape, 1) < 64
    return (
        jnp.where(low, first, pltpu.roll(second, 64, 1)),
        jnp.where(low, pltpu.roll(first, 64, 1), second),
    )


def survey(
    ids, records,
    slots, rows, places, count, seg_old, seg_face, seg_up, seg_store, seg_live, left, right,
    code_room, codes, sem,
):
    me = ids[1]
    lane = lax.broadcasted_iota(jnp.int32, (8, 128), 1)
    places_of = [pl.multiple_of(owner_of(k, me) * 56, 8) for k in range(8)]
    for k in range(8):
        code_room[k : k + 1] = records[pl.ds(places_of[k] + 48, 8), :][:1].astype(jnp.int32)
    copy = pltpu.make_async_copy(code_room, codes, sem)
    copy.start()

    for side, owner, row in ((left, (me + 7) & 7, 1), (right, (me + 1) & 7, 3)):
        columns = records[pl.ds(pl.multiple_of(owner * 56, 8) + 48, 8), :]
        side[0:128] = jnp.broadcast_to(columns[row : row + 1], (128, 128)).T
        side[128:160] = jnp.broadcast_to(columns[row + 1 : row + 2], (128, 128)).T[:32]

    copy.wait()

    def visit(slot, carry):
        n, live = carry
        for k in range(8):
            code = codes[k, slot]
            mine = (code >> 5) == me
            place = (slot & 1) * 64 + 8 * k + (slot >> 1)
            slots[n] = place
            rows[n] = code & 31
            places[n] = 16 * k + slot
            live = jnp.where(lane == jnp.where(mine, place, -1), 1.0, live)
            n = n + jnp.where(mine, 1, 0)
        return n, live

    n, live = lax.fori_loop(0, 16, visit, (jnp.int32(0), jnp.zeros((8, 128), F32)))
    seg_live[...] = live
    count[0] = (n + UNROLL - 1) // UNROLL
    for k in range(UNROLL - 1):
        slots[n + k] = -1
        rows[n + k] = 0
        places[n + k] = 0

    def field(k):
        return jnp.concatenate([records[pl.ds(p + 8 * k, 8), :] for p in places_of], axis=0)

    def turned(k):
        both = jnp.concatenate([field(k), field(k + 1)], axis=0).T
        return halves(both[:64], both[64:])

    seg_old[:64], seg_old[64:] = turned(0)
    trans, flags = turned(2)
    at = lax.broadcasted_iota(jnp.int32, (64, 128), 0)
    seg_face[:64] = jnp.where(at < 63, trans, 0.0)
    seg_face[64:] = jnp.where(at > 0, pltpu.roll(trans, 1, 0), 0.0)
    upstream = jnp.where(flags == 1.0, 1.0, 0.0)
    seg_up[:64] = upstream
    seg_up[64:] = 1.0 - pltpu.roll(upstream, 1, 0)
    seg_store[:64], seg_store[64:] = turned(4)


def collect(places, count, *refs):
    pieces, weights, sems = refs[:10], refs[10], refs[11]
    starts = (0, 16, 32, 40, 48, 64, 80, 96, 104, 112, 128)

    def fetch(i, carry):
        place = places[i]
        for k in range(10):

            @pl.when((place >= starts[k]) & (place < starts[k + 1]))
            def _():
                pltpu.make_async_copy(pieces[k].at[place - starts[k]], weights.at[i], sems.at[i]).start()

        return carry

    def settle(i, carry):
        pltpu.make_async_copy(pieces[0].at[0], weights.at[i], sems.at[i]).wait()
        return carry

    lax.fori_loop(0, count[0] * UNROLL, fetch, 0)
    lax.fori_loop(0, count[0] * UNROLL, settle, 0)


def survey_blocks(slots, rows, count, weights, lines, q, sums, returned, columns, levels):
    lane = lax.broadcasted_iota(jnp.int32, (64, 128), 1)
    sums[...] = jnp.zeros_like(sums)
    returned[...] = jnp.zeros_like(returned)
    columns[...] = jnp.zeros_like(columns)

    def body(step, carry):
        added = [jnp.zeros((64, 128), F32) for _ in range(4)]
        q_all = q[:64]
        backs = []
        for k in range(UNROLL):
            i = step * UNROLL + k
            slot, row = slots[i], rows[i]
            weight = weights[i]
            here = lane == slot
            for v in range(4):
                line = lines[pl.ds(32 * v + row, 1), :]
                total = jnp.sum(weight * line, axis=1, keepdims=True)
                added[v] = added[v] + jnp.where(here, total, 0.0)
            q_col = jnp.sum(jnp.where(here, q_all, 0.0), axis=1, keepdims=True)
            levels[i] = jnp.broadcast_to(q_col, (64, 128))
            back = jnp.sum(weight * q_col, axis=0, keepdims=True)
            valid = jnp.where(slot >= 0, 1.0, 0.0)
            backs.append((row, back, jnp.sum(weight, axis=0, keepdims=True) * valid))
        for v in range(4):
            sums[64 * v : 64 * v + 64] += added[v]
        for row, back, col in backs:
            returned[pl.ds(row, 1), :] += back
            columns[pl.ds(row, 1), :] += col
        return carry

    lax.fori_loop(0, count[0], body, 0)


def couple_blocks(slots, rows, count, weights, levels, lines, dq, inflow, returned):
    lane = lax.broadcasted_iota(jnp.int32, (64, 128), 1)
    returned[...] = jnp.zeros_like(returned)

    def body(step, carry):
        added = [jnp.zeros((64, 128), F32) for _ in range(2)]
        dq_all = dq[:64]
        backs = []
        for k in range(UNROLL):
            i = step * UNROLL + k
            slot, row = slots[i], rows[i]
            weight, level = weights[i], levels[i]
            here = lane == slot
            for v in range(2):
                first = lines[pl.ds(32 * v + row, 1), :]
                second = lines[pl.ds(64 + 32 * v + row, 1), :]
                total = jnp.sum(weight * (first - level * second), axis=1, keepdims=True)
                added[v] = added[v] + jnp.where(here, total, 0.0)
            dq_col = jnp.sum(jnp.where(here, dq_all, 0.0), axis=1, keepdims=True)
            backs.append((row, jnp.sum(weight * dq_col, axis=0, keepdims=True)))
        for v in range(2):
            inflow[64 * v : 64 * v + 64] += added[v]
        for row, back in backs:
            returned[pl.ds(row, 1), :] += back
        return carry

    lax.fori_loop(0, count[0], body, 0)


def combine(dots):
    total = jnp.broadcast_to(dots, (128, 128)).T
    gram = {}
    for n, (i, j) in enumerate(PAIRS):
        gram[i, j] = gram[j, i] = jnp.broadcast_to(total[n : n + 1, :], (8, 128))
    one = jnp.ones((8, 128), F32)
    remain = [one]
    factors = [jnp.zeros((8, 128), F32) for _ in range(SWEEPS)]
    for sweep in range(SWEEPS):
        image = [(j + 1, value / SCALE) for j, value in enumerate(remain)]
        cross = sum(value * factor * gram[j, i] for j, value in enumerate(remain) for i, factor in image)
        square = sum(a * b * gram[i, j] for i, a in image for j, b in image)
        alpha = cross / (square + TINY)
        for j, value in enumerate(remain):
            factors[j] = factors[j] + alpha * value
        longer = remain + [jnp.zeros((8, 128), F32)]
        for i, factor in image:
            longer[i] = longer[i] - alpha * factor
        remain = longer
    return factors


def spread(factor, rows):
    return jnp.broadcast_to(factor[:1], (rows, 128))


def summed(parts_ref):
    return jnp.sum(parts_ref[...], axis=0)


def face_terms(pres, satur, pres_across, satur_across, faces, own_up, coef_ref, stride):
    div_t = div_w = diag_t = diag_w = None
    count = len(pres_across)
    rows = pres.shape[0]
    for f in range(count):
        trans = faces[rows * f : rows * f + rows]
        up = own_up[rows * f : rows * f + rows]
        s_up = jnp.where(up == 1.0, satur, satur_across[f])
        drop = pres - pres_across[f]
        water, total = mobility(s_up)
        water_slope, total_slope = slopes(s_up)
        cond_t, cond_w = trans * total, trans * water
        lean = trans * drop
        at = rows * f
        coef_ref[at : at + rows] = cond_t
        coef_ref[stride + at : stride + at + rows] = cond_w
        coef_ref[2 * stride + at : 2 * stride + at + rows] = total_slope * lean
        coef_ref[3 * stride + at : 3 * stride + at + rows] = water_slope * lean
        flux_t, flux_w = cond_t * drop, cond_w * drop
        if f == 0:
            div_t, div_w, diag_t, diag_w = flux_t, flux_w, cond_t, cond_w
        else:
            div_t, div_w = div_t + flux_t, div_w + flux_w
            diag_t, diag_w = diag_t + cond_t, diag_w + cond_w
    return div_t, div_w, diag_t, diag_w


def face_tangents(dp, ds, dp_across, ds_across, own_up, coef, stride):
    rows = dp.shape[0]
    out_t = out_w = None
    for f in range(len(dp_across)):
        at = rows * f
        up = own_up[at : at + rows]
        drop = dp - dp_across[f]
        ds_up = jnp.where(up == 1.0, ds, ds_across[f])
        part_t = coef[at : at + rows] * drop + coef[2 * stride + at : 2 * stride + at + rows] * ds_up
        part_w = (
            coef[stride + at : stride + at + rows] * drop
            + coef[3 * stride + at : 3 * stride + at + rows] * ds_up
        )
        out_t = part_t if f == 0 else out_t + part_t
        out_w = part_w if f == 0 else out_w + part_w
    return out_t, out_w


def linearise(newton, *refs):
    refs = list(refs)

    def take(n):
        out = refs[:n]
        del refs[:n]
        return out

    slots, rows, count = take(3)
    cell_old, store, source, faces, own_up = take(5)
    seg_old, seg_store, seg_face, seg_up, seg_live, weights = take(6)
    [cell_in] = take(1)
    around = take(4)
    [seg_in] = take(1)
    if newton:
        [parts] = take(1)
        dir_cells = take(SWEEPS)
        dir_segs = take(SWEEPS)
        dir_around = [take(4) for _ in range(SWEEPS)]
    base_cell, base_seg, dir_cell, dir_seg = take(4)
    coef, seg_coef, lead, seg_lead, lines, reach, couple_rows, levels = take(8)
    if newton:
        cell_out, seg_out = take(2)
    inner_lines, sums, returned, columns = refs

    cell = cell_in[...]
    near = [r[0:64] for r in around]
    if newton:
        factors = combine(summed(parts))
        for j in range(SWEEPS):
            g = spread(factors[j], 64)
            cell = cell + g * dir_cells[j][...]
            near = [n + g * d[...] for n, d in zip(near, dir_around[j])]
        cell_out[...] = cell
        seg = seg_in[...]
        for j in range(SWEEPS):
            seg = seg + spread(factors[j], 128) * dir_segs[j][...]
        seg_out[...] = seg
        seg_ref = seg_out
    else:
        seg = seg_in[...]
        seg_ref = seg_in
    pres, satur = cell[:32], cell[32:]
    q, r = seg[:64], seg[64:]

    water, total = mobility(satur)
    water_slope, total_slope = slopes(satur)
    lines[0:32] = total
    lines[32:64] = water
    lines[64:96] = total_slope
    lines[96:128] = water_slope
    lines[128:160] = pres
    inner_lines[0:32] = total
    inner_lines[32:64] = water
    inner_lines[64:96] = total * pres
    inner_lines[96:128] = water * pres
    survey_blocks(slots, rows, count, weights, inner_lines, seg_ref, sums, returned, columns, levels)
    reach[...] = sums[0:128]
    column = columns[...]
    pull = pres * column - returned[...]
    couple_rows[0:32] = column
    couple_rows[32:64] = pull

    pres_across = neighbours(pres, *[n[:32] for n in near])
    satur_across = neighbours(satur, *[n[32:] for n in near])
    div_t, div_w, diag_t, diag_w = face_terms(
        pres, satur, pres_across, satur_across, faces, own_up, coef, 192
    )
    st, sw = store[:32], store[32:]
    moved = cell - cell_old[...]
    base_t = source[:32] - st * moved[:32] - div_t - total * pull
    base_w = source[32:] - sw * moved[32:] - div_w - water * pull
    lead_t = 1.0 / (st + diag_t)
    lead_w = 1.0 / sw
    lead[0:32] = lead_t
    lead[32:64] = diag_w
    lead[64:96] = lead_w
    base_cell[0:32] = base_t
    base_cell[32:64] = base_w
    first = base_t * lead_t
    dir_cell[0:32] = first
    dir_cell[32:64] = (base_w - diag_w * first) * lead_w

    chain_t, chain_w, chain_dt, chain_dw = face_terms(
        q, r, chain_neighbours(q), chain_neighbours(r), seg_face, seg_up, seg_coef, 128
    )
    live = jnp.broadcast_to(seg_live[:1], (64, 128))
    sst, ssw = seg_store[:64], seg_store[64:]
    shifted = seg - seg_old[...]
    inflow_t = sums[128:192] - q * sums[0:64]
    inflow_w = sums[192:256] - q * sums[64:128]
    seg_t = -live * (sst * shifted[:64] + chain_t - inflow_t)
    seg_w = -live * (ssw * shifted[64:] + chain_w - inflow_w)
    lead_t = 1.0 / (sst + chain_dt)
    lead_w = 1.0 / ssw
    seg_lead[0:64] = lead_t
    seg_lead[64:128] = chain_dw
    seg_lead[128:192] = lead_w
    base_seg[0:64] = seg_t
    base_seg[64:128] = seg_w
    first = seg_t * lead_t
    dir_seg[0:64] = first
    dir_seg[64:128] = (seg_w - chain_dw * first) * lead_w


def couple_dirs(
    slots, rows, count, dir_cell, dir_seg, lines, reach, weights, levels, inflow, returned, inner_lines
):
    dp, ds = dir_cell[:32], dir_cell[32:]
    pres = lines[128:160]
    lean_t = lines[64:96] * ds
    lean_w = lines[96:128] * ds
    inner_lines[0:32] = lines[0:32] * dp + lean_t * pres
    inner_lines[32:64] = lines[32:64] * dp + lean_w * pres
    inner_lines[64:96] = lean_t
    inner_lines[96:128] = lean_w
    dq = dir_seg[:64]
    inflow[0:64] = -dq * reach[0:64]
    inflow[64:128] = -dq * reach[64:128]
    couple_blocks(slots, rows, count, weights, levels, inner_lines, dir_seg, inflow, returned)


def advance(last, *refs):
    (
        dir_cell,
        below,
        above,
        left,
        right,
        dir_seg,
        inflow,
        returned,
        store,
        own_up,
        seg_store,
        seg_up,
        seg_live,
        coef,
        seg_coef,
        lead,
        seg_lead,
        lines,
        couple_rows,
    ) = refs[:19]
    next_cell, next_seg = refs[19:21]
    dp, ds = dir_cell[:32], dir_cell[32:]
    near = [n[...] for n in (below, above, left, right)]
    out_t, out_w = face_tangents(
        dp,
        ds,
        neighbours(dp, *[n[:32] for n in near]),
        neighbours(ds, *[n[32:] for n in near]),
        own_up,
        coef,
        192,
    )
    flow = dp * couple_rows[0:32] - returned[...]
    pull = ds * couple_rows[32:64]
    image_t = store[:32] * dp + out_t + lines[0:32] * flow + lines[64:96] * pull
    image_w = store[32:] * ds + out_w + lines[32:64] * flow + lines[96:128] * pull
    cell_t, cell_w = SCALE * image_t, SCALE * image_w
    next_cell[0:32] = cell_t
    next_cell[32:64] = cell_w

    dq, dr = dir_seg[:64], dir_seg[64:]
    chain_t, chain_w = face_tangents(
        dq, dr, chain_neighbours(dq), chain_neighbours(dr), seg_up, seg_coef, 128
    )
    live = jnp.broadcast_to(SCALE * seg_live[:1], (64, 128))
    seg_t = live * (seg_store[:64] * dq + chain_t - inflow[:64])
    seg_w = live * (seg_store[64:] * dr + chain_w - inflow[64:])
    next_seg[0:64] = seg_t
    next_seg[64:128] = seg_w
    if not last:
        next_dir, next_dir_seg = refs[21:23]
        first = cell_t * lead[0:32]
        next_dir[0:32] = first
        next_dir[32:64] = (cell_w - lead[32:64] * first) * lead[64:96]
        first = seg_t * seg_lead[0:64]
        next_dir_seg[0:64] = first
        next_dir_seg[64:128] = (seg_w - seg_lead[64:128] * first) * seg_lead[128:192]


def inner_products(*refs):
    cells, segs, out = refs[: SWEEPS + 1], refs[SWEEPS + 1 : 2 * SWEEPS + 2], refs[-1]
    lines = []
    for i, j in PAIRS:
        part = jnp.sum(cells[i][...] * cells[j][...], axis=0, keepdims=True)
        lines.append(part + jnp.sum(segs[i][...] * segs[j][...], axis=0, keepdims=True))
    lines.append(jnp.zeros((128 - len(PAIRS), 128), F32))
    total = jnp.sum(jnp.concatenate(lines, axis=0).T, axis=0, keepdims=True)
    out[...] = jnp.broadcast_to(total[None], out.shape)


def address(*refs):
    ids, seg, seg_old = refs[:3]
    dir_segs, out = refs[3 : 3 + SWEEPS], refs[-1]
    me = ids[1]
    fields = [seg[...] - seg_old[...]] + [d[...] for d in dir_segs]
    for n, field in enumerate(fields):
        turned = jnp.concatenate(halves(field[:64], field[64:]), axis=0).T
        for k in range(8):
            owner = owner_of(k, me)
            out[owner, 16 * n : 16 * n + 8] = turned[8 * k : 8 * k + 8]
            out[owner, 16 * n + 8 : 16 * n + 16] = turned[64 + 8 * k : 64 + 8 * k + 8]


def finish(*refs):
    parts, cell, home = refs[:3]
    dir_cells = refs[3 : 3 + SWEEPS]
    cell_out, moved = refs[3 + SWEEPS :]
    factors = combine(summed(parts))
    total = cell[...]
    arrived = jnp.sum(home[...], axis=0)
    shift = arrived[0:16]
    for j in range(SWEEPS):
        total = total + spread(factors[j], 64) * dir_cells[j][...]
        shift = shift + spread(factors[j], 16) * arrived[16 * j + 16 : 16 * j + 32]
    cell_out[...] = total
    moved[...] = shift


def ring(block, axis, distance):
    count = lax.axis_size(axis)
    return lax.ppermute(block, axis, [(i, (i + distance) % count) for i in range(count)])


def swapped(block, axis):
    return lax.ppermute(block, axis, [(i, i ^ 1) for i in range(lax.axis_size(axis))])


def exchanged(block):
    left, right = ring(block, "frac", 1), ring(block, "frac", -1)
    return [ring(block, "region", 1), ring(block, "region", -1), left, right]


def after(first, *others):
    return lax.optimization_barrier((first, *others))


def on_device(
    pres_old,
    satur_old,
    permeability,
    storage,
    source,
    face_upwind,
    frac_pres_old,
    frac_satur_old,
    frac_storage,
    frac_trans,
    frac_upwind,
    coupling,
    target_part,
    target_row,
    live_count,
):
    blocks = coupling.shape[0]
    ids = jnp.stack(
        [
            lax.axis_index("region"),
            lax.axis_index("frac"),
            jnp.int32(lax.axis_size("region")),
            jnp.int32(lax.axis_size("frac")),
        ]
    ).astype(jnp.int32)
    one_right = ring(coupling, "frac", 2)
    one_left = ring(coupling, "frac", -2)
    ids, message, record, cell_old, flag_y = call(
        pack,
        [smem_i32(4), vmem(160, 128), vmem(8, 56, 128), vmem(64, 128), vmem(32, 128)],
        [
            ids,
            target_part,
            target_row,
            live_count,
            pres_old,
            satur_old,
            permeability,
            face_upwind,
            frac_pres_old.reshape(8, 128),
            frac_satur_old.reshape(8, 128),
            frac_trans.reshape(8, 128),
            frac_upwind.reshape(8, 128),
            frac_storage,
        ],
        "ssss" + "H" * 9,
        out_spaces="svvvv",
        scratch=[
            vmem(56, 128),
            pltpu.VMEM((3, 1, 32, 128), jnp.int32),
            pltpu.VMEM((8, 128), jnp.int32),
            pltpu.VMEM((2, 1024), F32),
            pltpu.SemaphoreType.DMA((9,)),
        ],
        name="pack",
    )
    records = lax.all_to_all(record, "frac", 0, 0).reshape(448, 128)
    one_right, one_left, records = after(one_right, one_left, records)
    below, above = ring(message, "region", 1), ring(message, "region", -1)
    half = blocks // 2
    two = [ring(one_right[:half], "frac", 2), ring(one_left[half:], "frac", -2)]
    same = [coupling, one_right, *two, one_left]
    pieces = same + [swapped(x, "frac") for x in same]
    room = 8 * blocks + UNROLL
    slots, rows, places, count, seg_old, seg_face, seg_up, seg_store, seg_live, left, right = call(
        survey,
        [
            smem_i32(room),
            smem_i32(room),
            smem_i32(room),
            smem_i32(1),
            vmem(128, 128),
            vmem(128, 128),
            vmem(128, 128),
            vmem(128, 128),
            vmem(8, 128),
            vmem(160, 128),
            vmem(160, 128),
        ],
        [ids, records],
        "Sv",
        out_spaces="ssss" + "v" * 7,
        scratch=[
            pltpu.VMEM((8, 128), jnp.int32),
            pltpu.SMEM((8, 128), jnp.int32),
            pltpu.SemaphoreType.DMA,
        ],
        flops=6_000_000,
        name="survey",
    )
    around = [below, above, left, right]
    faces, own_up = call(
        geometry,
        [vmem(192, 128), vmem(192, 128)],
        [ids, message, *around, flag_y],
        "Svvvvvv",
        flops=2_000_000,
        name="geometry",
    )
    [weights] = call(
        collect,
        [vmem(room, 64, 128)],
        [places, count, *pieces],
        "SSH" + "a" * 9,
        scratch=[pltpu.SemaphoreType.DMA((room,))],
        name="collect",
    )
    lists = [slots, rows, count]
    store = storage.reshape(64, 128)
    wells = source.reshape(64, 128)
    inner = [vmem(128, 128), vmem(256, 128)]
    devices = lax.axis_size("region") * lax.axis_size("frac")

    cell, seg = cell_old, seg_old
    near = around
    parts = None
    for newton in range(NEWTON):
        args = [
            *lists,
            cell_old,
            store,
            wells,
            faces,
            own_up,
            seg_old,
            seg_store,
            seg_face,
            seg_up,
            seg_live,
            weights,
            cell,
            *near,
            seg,
        ]
        outs = [
            vmem(64, 128),
            vmem(128, 128),
            vmem(64, 128),
            vmem(128, 128),
            vmem(768, 128),
            vmem(512, 128),
            vmem(96, 128),
            vmem(192, 128),
            vmem(160, 128),
            vmem(128, 128),
            vmem(64, 128),
            vmem(room, 64, 128),
        ]
        if newton:
            args += [parts, *dir_cells, *dir_segs, *[x for group in dir_around for x in group]]
            outs += [vmem(64, 128), vmem(128, 128)]
        made = call(
            lambda *refs, newton=newton: linearise(newton, *refs),
            outs,
            args,
            "SSS" + "v" * (len(args) - 3),
            scratch=[*inner, vmem(32, 128), vmem(32, 128)],
            name="linearise",
        )
        base_cell, base_seg, dir_cell, dir_seg = made[:4]
        coef, seg_coef, lead, seg_lead, lines, reach, couple_rows, levels = made[4:12]
        if newton:
            cell, seg = made[12:]
        base_cells, base_segs = [base_cell], [base_seg]
        dir_cells, dir_segs, dir_around = [], [], []
        for sweep in range(SWEEPS):
            last = sweep == SWEEPS - 1
            nearby = exchanged(dir_cell)
            inflow, returned = call(
                couple_dirs,
                [vmem(128, 128), vmem(32, 128)],
                [*lists, dir_cell, dir_seg, lines, reach, weights, levels],
                "SSS" + "v" * 6,
                scratch=inner[:1],
                name="couple",
            )
            dir_cells.append(dir_cell)
            dir_segs.append(dir_seg)
            dir_around.append(nearby)
            args = [
                dir_cell,
                *nearby,
                dir_seg,
                inflow,
                returned,
                store,
                own_up,
                seg_store,
                seg_up,
                seg_live,
                coef,
                seg_coef,
                lead,
                seg_lead,
                lines,
                couple_rows,
            ]
            if last and newton == NEWTON - 1:
                inflow, seg_now = after(inflow, seg)
                [home] = call(
                    address,
                    [vmem(8, 16 * SWEEPS + 16, 128)],
                    [ids, seg_now, seg_old, *dir_segs],
                    "S" + "v" * (2 + SWEEPS),
                    name="address",
                )
                home = lax.all_to_all(home, "frac", 0, 0)
            made = call(
                lambda *refs, last=last: advance(last, *refs),
                [vmem(64, 128), vmem(128, 128)] * (1 if last else 2),
                args,
                "v" * len(args),
                name="advance",
            )
            if last and newton == NEWTON - 1:
                made = list(after(*made, home))
                home = made.pop()
            base_cells.append(made[0])
            base_segs.append(made[1])
            if not last:
                dir_cell, dir_seg = made[2:]
        [parts] = call(
            inner_products,
            [vmem(devices, 1, 128)],
            [*base_cells, *base_segs],
            "v" * (2 * SWEEPS + 2),
            name="inner_products",
        )
        parts = lax.all_to_all(parts, ("region", "frac"), 0, 0)

    args = [parts, cell, home, *dir_cells]
    cell_state, moved = call(
        finish,
        [jax.ShapeDtypeStruct((64, 128), F32), vmem(16, 128)],
        args,
        "v" * len(args),
        name="finish",
    )
    seg_state = jnp.stack([frac_pres_old, frac_satur_old]) + moved.reshape(2, -1)
    return (cell_state.reshape(2, 1, 32, 128), seg_state)


def solution(mesh):
    placed = (
        P("region", None, "frac"),
        P("region", None, "frac"),
        P("region", None, "frac"),
        P(None, "region", None, "frac"),
        P(None, "region", None, "frac"),
        P(None, "region", None, "frac"),
        P(("region", "frac")),
        P(("region", "frac")),
        P(None, ("region", "frac")),
        P(("region", "frac")),
        P(("region", "frac")),
        P(("region", "frac"), None, None),
        P(("region", "frac")),
        P(("region", "frac")),
        P(("region", "frac")),
    )
    return jax.shard_map(
        on_device,
        mesh=mesh,
        in_specs=placed,
        out_specs=(P(None, "region", None, "frac"), P(None, ("region", "frac"))),
        check_vma=False,
    )
```
